128 devices in a mesh: gr: 8 (over y_hi, z), gc: 16 (over x, y_lo, core).
Axes of the slice: x: 4, y: 4 (y_hi: 2, y_lo: 2; y = y_hi * 2 + y_lo), z: 4, core: 2. Of those that a mesh axis runs over, the one named last changes fastest.
Arguments:
- items: bfloat16 [16384, 4096], P(('gr', 'gc'))
- position_of: int32 [16384], P(('gr', 'gc')), may hold values from 0 to 16383, as said below
Outputs:
- similarity: bfloat16 [16384, 16384], P('gr', 'gc')
- best_other: float32 [16384], P('gr')
The draws below stay inside these ranges and needn't reach their ends.
Inputs may be any that keep to these rules, and one draw needn't show every extreme that they name: `position_of`: A permutation. Position p has home device p // 128 in the order gr+gc; the items of device s go to home devices s * 128, s * 128 + 1, ... taken modulo 128, so each device sends at most 1 items to each home device and each home device receives 128.
All inputs are finite; a program needn't handle non-finite values.
Results may differ from the reference program's by a relative error of at most 0.001.
Values may be sent and summed in bfloat16 or wider, within the bound.
No kernel may reach another device: no remote copies, remote signals or barrier semaphores. Data moves between devices by JAX's collectives and lax.ppermute only.
A program may use at most 128 MiB of HBM per device.

```python
import jax
import jax.numpy as jnp
from jax import lax

EMBED = 4096
ITEMS_DEV = 128
SHARDS = 128
ITEMS = 16384
ROWS_DEV = 2048
N_GR = 8
N_GC = 16


def draw_items(key, part):
    key = jax.random.fold_in(key, 11)
    key_z, key_r, key_c = jax.random.split(key, 3)
    row_scale = jnp.exp(jax.random.uniform(key_r, (ITEMS, 1), jnp.float32, 0.0, 2.4))
    col_scale = jnp.exp(jax.random.uniform(key_c, (1, EMBED), jnp.float32, -0.7, 1.1))
    noise = jax.random.normal(key_z, (ITEMS, EMBED), jnp.float32)
    values = row_scale * (noise * col_scale)
    return values.astype(jnp.bfloat16)


def draw_position_of(key, part):
    key = jax.random.fold_in(key, 23)
    key_a, key_b = jax.random.split(key)
    source_keys = jax.random.split(key_a, SHARDS)
    home_keys = jax.random.split(key_b, SHARDS)
    order = jax.vmap(lambda k: jax.random.permutation(k, ITEMS_DEV))(source_keys).astype(jnp.int32)
    arrival_slot = jax.vmap(lambda k: jax.random.permutation(k, ITEMS_DEV))(home_keys).astype(jnp.int32)
    source = jnp.arange(SHARDS, dtype=jnp.int32)[:, None]
    within = jnp.arange(ITEMS_DEV, dtype=jnp.int32)[None, :]
    overall = source * ITEMS_DEV + within
    home = overall % SHARDS
    arrival = overall // SHARDS
    position = home * ITEMS_DEV + arrival_slot[home.reshape(-1), arrival.reshape(-1)].reshape(SHARDS, ITEMS_DEV)
    item_id = source * ITEMS_DEV + order
    return jnp.zeros((ITEMS,), jnp.int32).at[item_id.reshape(-1)].set(position.reshape(-1))


def setup_inputs(seed: int = 0) -> dict:
    streams_of = jax.random.split(jax.random.key(seed), 3)
    items = draw_items(jax.random.fold_in(streams_of[2], 71), 0)
    position_of = draw_position_of(jax.random.fold_in(streams_of[2], 71), 0)
    return dict(items=items, position_of=position_of)


def inverse_norm(block):
    wide = block.astype(jnp.float32)
    return 1.0 / jnp.sqrt(lax.optimization_barrier(jnp.sum(wide * wide, axis=1)) + 1e-06)

def reference(items, position_of):
    total = items.shape[0]
    holder = jnp.zeros((total,), jnp.int32).at[position_of].set(jnp.arange(total, dtype=jnp.int32))
    placed = items[holder]
    columns = placed.reshape(N_GR, N_GC, ITEMS_DEV, EMBED).transpose(1, 0, 2, 3).reshape(total, EMBED)
    col_pos = jnp.arange(total, dtype=jnp.int32).reshape(N_GR, N_GC, ITEMS_DEV).transpose(1, 0, 2).reshape(total)
    row_inv = inverse_norm(placed)
    col_inv = inverse_norm(columns)

    def one_block(index):
        start = (index * ROWS_DEV).astype(jnp.int32)
        rows = lax.dynamic_slice_in_dim(placed, start, ROWS_DEV, 0)
        rinv = lax.dynamic_slice_in_dim(row_inv, start, ROWS_DEV, 0)
        product = lax.dot_general(rows, columns, (((1,), (1,)), ((), ())), preferred_element_type=jnp.float32)
        scaled = product * rinv[:, None] * col_inv[None, :]
        row_pos = start + jnp.arange(ROWS_DEV, dtype=jnp.int32)
        masked = jnp.where(col_pos[None, :] == row_pos[:, None], jnp.float32(-2.0), scaled)
        return (scaled.astype(jnp.bfloat16), lax.optimization_barrier(jnp.max(masked, axis=1)))
    sims, best = lax.map(one_block, jnp.arange(N_GR, dtype=jnp.int32))
    return (sims.reshape(total, total), best.reshape(total))
```

```python
import jax
import jax.numpy as jnp
from jax import lax
from jax.experimental import pallas as pl
from jax.experimental.pallas import tpu as pltpu
from jax.sharding import PartitionSpec as P

AXES = ("gr", "gc")
SIZES = {"yh": 2, "z": 4, "x": 4, "yl": 2, "c": 2}
F32 = jnp.float32
BF16 = jnp.bfloat16
MIB = 1024 * 1024


def coords(d):
    gr, gc = divmod(d, 16)
    return {"yh": gr // 4, "z": gr % 4, "x": gc // 4, "yl": (gc // 2) % 2, "c": gc % 2}


def flat(c):
    return (c["yh"] * 4 + c["z"]) * 16 + c["x"] * 4 + c["yl"] * 2 + c["c"]


def shift(value, **by):
    pairs = []
    for d in range(128):
        c = coords(d)
        for k, v in by.items():
            c[k] = (c[k] + v) % SIZES[k]
        pairs.append((d, flat(c)))
    return lax.ppermute(value, AXES, pairs)


def pack_kernel(pos_ref, items_ref, out_ref):
    count, width = items_ref.shape
    pos = pos_ref[...]
    dest = lax.broadcasted_iota(jnp.int32, (count, count), 0)
    hit = (pos // count) == dest
    pick = jnp.where(hit, 1.0, 0.0).astype(BF16)
    step = 1024
    for s in range(0, width, step):
        out_ref[:, s : s + step] = jnp.dot(
            pick, items_ref[:, s : s + step], preferred_element_type=F32
        ).astype(BF16)
    slot = jnp.sum(jnp.where(hit, (pos % count).astype(F32), 0.0), axis=1, keepdims=True)
    out_ref[:, width:] = jnp.broadcast_to(slot, (count, 128)).astype(BF16)


def place_kernel(in_ref, out_ref):
    count, width = out_ref.shape
    slot = in_ref[:, width:].astype(F32)
    lane = lax.broadcasted_iota(jnp.int32, (count, count), 1).astype(F32)
    pick = jnp.where(slot == lane, 1.0, 0.0).astype(BF16)
    step = 1024
    for s in range(0, width, step):
        out_ref[:, s : s + step] = lax.dot_general(
            pick, in_ref[:, s : s + step], (((0,), (0,)), ((), ())), preferred_element_type=F32
        ).astype(BF16)


def inverse_norm(ref, start, rows):
    total = jnp.zeros((rows, 128), F32)
    for s in range(0, ref.shape[1], 128):
        part = ref[start : start + rows, s : s + 128].astype(F32)
        total = total + part * part
    return 1.0 / jnp.sqrt(jnp.sum(total, axis=1, keepdims=True) + 1e-06)


def across(column):
    return jnp.transpose(jnp.broadcast_to(column, (128, 128)))[:1, :]


def make_block_kernel(row_parts, col_parts, first):
    n_rp, n_cp = len(row_parts), len(col_parts)
    n_rows = sum(row_parts)
    n_cols = sum(col_parts)
    rb, cb = n_rows // 128, n_cols // 128
    tile = 512

    def kernel(*refs):
        refs = list(refs)
        where = refs.pop(0)
        row_refs = [refs.pop(0) for _ in range(n_rp)]
        col_refs = [refs.pop(0) for _ in range(n_cp)]
        best_in = None if first else refs.pop(0)
        if not first:
            refs.pop(0)
        out_ref, best_out, rows_v, cols_v, stage, row_sem, col_sem, out_sem = refs
        if first:
            best_out[...] = jnp.full(best_out.shape, -2.0, F32)
        else:
            best_out[...] = best_in[...]

        def loads(parts, sources, target, sems):
            at, made = 0, []
            for n, (size, src) in enumerate(zip(parts, sources)):
                made.append((at, pltpu.make_async_copy(src, target.at[pl.ds(at, size)], sems.at[n])))
                at += size
            return made

        col_loads = loads(col_parts, col_refs, cols_v, col_sem)
        row_loads = loads(row_parts, row_refs, rows_v, row_sem)
        for _, c in col_loads:
            c.start()
        for _, c in row_loads:
            c.start()
        for _, c in col_loads:
            c.wait()
        col_inv = jnp.concatenate(
            [across(inverse_norm(cols_v, 128 * b, 128)) for b in range(cb)], axis=1
        )
        stores = {}
        for t in range(n_rows // tile):
            base = t * tile
            for at, c in row_loads:
                if base <= at < base + tile:
                    c.wait()
            held = t % 2
            if t >= 2:
                for c in stores[t - 2]:
                    c.wait()
            product = lax.dot_general(
                rows_v[base : base + tile, :],
                cols_v[...],
                (((1,), (1,)), ((), ())),
                preferred_element_type=F32,
            )
            stores[t] = []
            for k in range(tile // 128):
                r = t * (tile // 128) + k
                scaled = (
                    product[128 * k : 128 * k + 128, :]
                    * inverse_norm(rows_v, base + 128 * k, 128)
                    * col_inv
                )
                stage[held, 128 * k : 128 * k + 128, :] = scaled.astype(BF16)
                if first and r == 0:
                    lane = lax.broadcasted_iota(jnp.int32, scaled.shape, 1)
                    sub = lax.broadcasted_iota(jnp.int32, scaled.shape, 0)
                    scaled = jnp.where(lane == sub, -2.0, scaled)
                top = across(jnp.max(scaled, axis=1, keepdims=True))
                a = where[r]
                best_out[pl.ds(a, 1), :] = jnp.maximum(best_out[pl.ds(a, 1), :], top)
                for b in range(cb):
                    c = pltpu.make_async_copy(
                        stage.at[held, pl.ds(128 * k, 128), pl.ds(128 * b, 128)],
                        out_ref.at[
                            pl.ds(pl.multiple_of(a * 128, 128), 128),
                            pl.ds(pl.multiple_of(where[rb + b] * 128, 128), 128),
                        ],
                        out_sem.at[held, k * cb + b],
                    )
                    c.start()
                    stores[t].append(c)
        for t in range(max(0, n_rows // tile - 2), n_rows // tile):
            for c in stores[t]:
                c.wait()

    return kernel


def block_call(row_parts, rows_at, col_parts, cols_at, state):
    first = state is None
    row_sizes = [p.shape[0] for p in row_parts]
    col_sizes = [p.shape[0] for p in col_parts]
    n_rows, n_cols = sum(row_sizes), sum(col_sizes)
    width = row_parts[0].shape[1]
    where = jnp.stack(list(rows_at) + list(cols_at)).astype(jnp.int32)
    args = [where, *row_parts, *col_parts]
    any_spec = pl.BlockSpec(memory_space=pl.ANY)
    vmem_spec = pl.BlockSpec(memory_space=pltpu.VMEM)
    in_specs = [pl.BlockSpec(memory_space=pltpu.SMEM)] + [any_spec] * (len(args) - 1)
    aliases = {}
    if not first:
        out, best = state
        args += [best, out]
        in_specs += [vmem_spec, any_spec]
        aliases = {len(args) - 1: 0}
    tile = 512
    return pl.pallas_call(
        make_block_kernel(row_sizes, col_sizes, first),
        out_shape=(
            jax.ShapeDtypeStruct((2048, 1024), BF16),
            jax.ShapeDtypeStruct((16, 128), F32),
        ),
        in_specs=in_specs,
        out_specs=(any_spec, vmem_spec),
        input_output_aliases=aliases,
        scratch_shapes=[
            pltpu.VMEM((n_rows, width), BF16),
            pltpu.VMEM((n_cols, width), BF16),
            pltpu.VMEM((2, tile, n_cols), BF16),
            pltpu.SemaphoreType.DMA((len(row_sizes),)),
            pltpu.SemaphoreType.DMA((len(col_sizes),)),
            pltpu.SemaphoreType.DMA((2, tile // 128 * (n_cols // 128))),
        ],
        compiler_params=pltpu.CompilerParams(vmem_limit_bytes=40 * MIB),
        cost_estimate=pl.CostEstimate(
            flops=2 * n_rows * n_cols * width,
            bytes_accessed=2 * width * (n_rows + n_cols) + 2 * n_rows * n_cols,
            transcendentals=0,
        ),
    )(*args)


def per_device(items, position_of):
    count, width = items.shape
    vmem_spec = pl.BlockSpec(memory_space=pltpu.VMEM)
    send = pl.pallas_call(
        pack_kernel,
        out_shape=jax.ShapeDtypeStruct((count, width + 128), BF16),
        in_specs=[vmem_spec, vmem_spec],
        out_specs=vmem_spec,
    )(position_of.reshape(1, count), items)
    arrived = lax.all_to_all(send, AXES, split_axis=0, concat_axis=0, tiled=True)
    own = pl.pallas_call(
        place_kernel,
        out_shape=jax.ShapeDtypeStruct((count, width), BF16),
        in_specs=[vmem_spec],
        out_specs=vmem_spec,
    )(arrived)

    gr, gc = lax.axis_index("gr"), lax.axis_index("gc")
    yh, z = gr // 4, gr % 4
    x, yl, core = gc // 4, (gc // 2) % 2, gc % 2

    def row_at(dx=0, dy=0, dc=0):
        return ((x + dx) % 4) * 4 + ((yl + dy) % 2) * 2 + (core + dc) % 2

    def col_at(dy=0, dz=0):
        return ((yh + dy) % 2) * 4 + (z + dz) % 4

    half = count // 2
    pair = shift(own, yl=1)
    x_up, x_dn = shift(own, x=1), shift(own, x=-1)
    z_up, z_dn = shift(own, z=1), shift(own, z=-1)
    own_c = shift(own, c=1)
    far = shift(pair, yh=1, yl=1)
    x2_a, x2_b = shift(x_up[:half], x=1), shift(x_dn[half:], x=-1)
    z2_a, z2_b = shift(z_up[:half], z=1), shift(z_dn[half:], z=-1)
    px_up, px_dn = shift(pair, x=1), shift(pair, x=-1)
    pair_c, x_up_c, x_dn_c = shift(pair, c=1), shift(x_up, c=1), shift(x_dn, c=1)
    fz_up, fz_dn = shift(far, z=1), shift(far, z=-1)
    px2_a, px2_b = shift(x2_a, yl=1), shift(x2_b, yl=1)
    x2_ac, x2_bc = shift(x2_a, c=1), shift(x2_b, c=1)
    px_up_c, px_dn_c = shift(px_up, c=1), shift(px_dn, c=1)
    fz2_a, fz2_b = shift(fz_up[:half], z=1), shift(fz_dn[half:], z=-1)
    px2_ac, px2_bc = shift(px2_a, c=1), shift(px2_b, c=1)

    rows_1 = [own, own_c, pair, pair_c, x_up, x_up_c, x_dn, x_dn_c]
    at_1 = [
        row_at(), row_at(dc=1), row_at(dy=1), row_at(dy=1, dc=1),
        row_at(-1), row_at(-1, dc=1), row_at(1), row_at(1, dc=1),
    ]
    rows_2 = [px_up, px_up_c, px_dn, px_dn_c, x2_a, x2_b, x2_ac, x2_bc, px2_a, px2_b, px2_ac, px2_bc]
    at_2 = [
        row_at(-1, 1), row_at(-1, 1, 1), row_at(1, 1), row_at(1, 1, 1),
        row_at(2), row_at(2, dc=1), row_at(2, 1), row_at(2, 1, 1),
    ]
    cols_1 = [own, z_up, z_dn, z2_a, z2_b]
    cat_1 = [col_at(), col_at(dz=-1), col_at(dz=1), col_at(dz=2)]
    cols_2 = [fz_up, fz_dn]
    cat_2 = [col_at(1, -1), col_at(1, 1)]
    cols_3 = [far, fz2_a, fz2_b]
    cat_3 = [col_at(1), col_at(1, 2)]

    state = block_call(rows_1, at_1, cols_1, cat_1, None)
    state = block_call(rows_2, at_2, cols_1, cat_1, state)
    state = block_call(rows_1 + rows_2, at_1 + at_2, cols_2, cat_2, state)
    out, best = block_call(rows_1 + rows_2, at_1 + at_2, cols_3, cat_3, state)

    best = jnp.maximum(best, shift(best, c=1))
    best = jnp.maximum(best, shift(best, yl=1))
    best = jnp.maximum(
        jnp.maximum(best, shift(best, x=2)), jnp.maximum(shift(best, x=1), shift(best, x=-1))
    )
    return out, best.reshape(-1)


def solution(mesh):
    return jax.shard_map(
        per_device,
        mesh=mesh,
        in_specs=(P(("gr", "gc"), None), P(("gr", "gc"))),
        out_specs=(P("gr", "gc"), P("gr")),
        check_vma=False,
    )
```

```python
import jax
import jax.numpy as jnp
from jax import lax
from jax.experimental import pallas as pl
from jax.experimental.pallas import tpu as pltpu
from jax.sharding import PartitionSpec as P

AXES = ("gr", "gc")
SIZES = {"yh": 2, "z": 4, "x": 4, "yl": 2, "c": 2}
F32 = jnp.float32
BF16 = jnp.bfloat16
MIB = 1024 * 1024


def coords(d):
    gr, gc = divmod(d, 16)
    return {"yh": gr // 4, "z": gr % 4, "x": gc // 4, "yl": (gc // 2) % 2, "c": gc % 2}


def flat(c):
    return (c["yh"] * 4 + c["z"]) * 16 + c["x"] * 4 + c["yl"] * 2 + c["c"]


def send(value, route):
    pairs = []
    for d in range(128):
        c = coords(d)
        for k, v in route.items():
            step = (1 if c["c"] == 0 else -1) if v == "ring" else v
            c[k] = (c[k] + step) % SIZES[k]
        pairs.append((d, flat(c)))
    return lax.ppermute(value, AXES, pairs)


def pack_kernel(pos_ref, items_ref, out_ref):
    count, width = items_ref.shape
    pos = pos_ref[...]
    dest = lax.broadcasted_iota(jnp.int32, (count, count), 0)
    hit = (pos // count) == dest
    pick = jnp.where(hit, 1.0, 0.0).astype(BF16)
    step = 1024
    for s in range(0, width, step):
        out_ref[:, s : s + step] = jnp.dot(
            pick, items_ref[:, s : s + step], preferred_element_type=F32
        ).astype(BF16)
    slot = jnp.sum(jnp.where(hit, (pos % count).astype(F32), 0.0), axis=1, keepdims=True)
    out_ref[:, width:] = jnp.broadcast_to(slot, (count, 128)).astype(BF16)


def place_kernel(in_ref, out_ref, low_ref, high_ref):
    count, width = out_ref.shape
    slot = in_ref[:, width:].astype(F32)
    lane = lax.broadcasted_iota(jnp.int32, (count, count), 1).astype(F32)
    pick = jnp.where(slot == lane, 1.0, 0.0).astype(BF16)
    step = 1024
    for s in range(0, width, step):
        out_ref[:, s : s + step] = lax.dot_general(
            pick, in_ref[:, s : s + step], (((0,), (0,)), ((), ())), preferred_element_type=F32
        ).astype(BF16)
    low_ref[...] = out_ref[: count // 2, :]
    high_ref[...] = out_ref[count // 2 :, :]


def join_kernel(low_ref, high_ref, out_ref, sems):
    half = low_ref.shape[0]
    copies = [
        pltpu.make_async_copy(src, out_ref.at[pl.ds(half * n, half)], sems.at[n])
        for n, src in enumerate((low_ref, high_ref))
    ]
    for c in copies:
        c.start()
    for c in copies:
        c.wait()


def join(low, high):
    any_spec = pl.BlockSpec(memory_space=pl.ANY)
    return pl.pallas_call(
        join_kernel,
        out_shape=jax.ShapeDtypeStruct((2 * low.shape[0], low.shape[1]), BF16),
        in_specs=[any_spec, any_spec],
        out_specs=pl.BlockSpec(memory_space=pltpu.VMEM),
        scratch_shapes=[pltpu.SemaphoreType.DMA((2,))],
        compiler_params=pltpu.CompilerParams(vmem_limit_bytes=2 * MIB),
    )(low, high)


def inverse_norm(ref, start, rows):
    total = jnp.zeros((rows, 128), F32)
    for s in range(0, ref.shape[1], 128):
        part = ref[start : start + rows, s : s + 128].astype(F32)
        total = total + part * part
    return 1.0 / jnp.sqrt(jnp.sum(total, axis=1, keepdims=True) + 1e-06)


def across(column):
    return jnp.transpose(jnp.broadcast_to(column, (128, 128)))[:1, :]


def make_block_kernel(n_rb, n_cb, fresh_rows, fresh_cols, diagonal, last):
    tile = 512 if fresh_rows else 1024
    per_tile = tile // 128

    def kernel(*refs):
        refs = list(refs)
        where = refs.pop(0)
        n_rows = [refs.pop(0) for _ in range(n_rb if fresh_rows else 2)]
        n_cols = [refs.pop(0) for _ in range(n_cb if fresh_cols else 1)]
        row_inv = None if fresh_rows else [refs.pop(0), refs.pop(0)]
        col_inv = None if fresh_cols else refs.pop(0)
        best_in = None if fresh_rows else [refs.pop(0), refs.pop(0)]
        if not diagonal:
            refs.pop(0)
        out_ref = refs.pop(0)
        final_ref = refs.pop(0) if last else None
        best_out = [refs.pop(0)] if fresh_rows or last else [refs.pop(0), refs.pop(0)]
        rows_v = refs.pop(0) if fresh_rows else None
        row_inv_out = refs.pop(0) if fresh_rows else None
        cols_v = refs.pop(0) if fresh_cols else n_cols[0]
        if fresh_cols:
            col_inv = refs.pop(0)
        row_sem, col_sem, out_sem = refs

        col_loads, row_loads = [], []
        if fresh_cols:
            for n, src in enumerate(n_cols):
                c = pltpu.make_async_copy(src, cols_v.at[pl.ds(128 * n, 128)], col_sem.at[n])
                c.start()
                col_loads.append(c)
        if fresh_rows:
            for n, src in enumerate(n_rows):
                c = pltpu.make_async_copy(src, rows_v.at[pl.ds(128 * n, 128)], row_sem.at[n])
                c.start()
                row_loads.append(c)
        for n, c in enumerate(col_loads):
            c.wait()
            col_inv[:, 128 * n : 128 * n + 128] = jnp.broadcast_to(
                across(inverse_norm(cols_v, 128 * n, 128)), (8, 128)
            )
        stores = []
        n_tiles = n_rb // per_tile
        for t in range(n_tiles):
            if fresh_rows:
                for c in row_loads[t * per_tile : (t + 1) * per_tile]:
                    c.wait()
                source, at = rows_v, t * tile
                part, at_r = None, t * tile
            else:
                part, at_r = divmod(t * tile, 1024)
                source, at = n_rows[part], at_r
            product = lax.dot_general(
                source[at : at + tile, :],
                cols_v[...],
                (((1,), (1,)), ((), ())),
                preferred_element_type=F32,
            )
            for k in range(per_tile):
                r = t * per_tile + k
                span = slice(at_r + 128 * k, at_r + 128 * k + 128)
                if fresh_rows:
                    inv = jnp.broadcast_to(
                        inverse_norm(rows_v, at_r + 128 * k, 128), (128, 128)
                    )
                    row_inv_out[span, :] = inv
                    top = None
                else:
                    inv = row_inv[part][span, :]
                    top = best_in[part][span, :]
                a = where[r]
                here = pl.ds(pl.multiple_of(a * 128, 128), 128)
                for b in range(n_cb):
                    lanes = slice(128 * b, 128 * b + 128)
                    scaled = product[128 * k : 128 * k + 128, lanes] * inv * col_inv[:1, lanes]
                    out_ref[
                        here, pl.ds(pl.multiple_of(where[n_rb + b] * 128, 128), 128)
                    ] = scaled.astype(BF16)
                    if diagonal and r == 0 and b == 0:
                        lane = lax.broadcasted_iota(jnp.int32, scaled.shape, 1)
                        sub = lax.broadcasted_iota(jnp.int32, scaled.shape, 0)
                        scaled = jnp.where(lane == sub, -2.0, scaled)
                    top = scaled if top is None else jnp.maximum(top, scaled)
                if last:
                    best_out[0][pl.ds(a, 1), :] = across(jnp.max(top, axis=1, keepdims=True))
                    c = pltpu.make_async_copy(
                        out_ref.at[here, :], final_ref.at[here, :], out_sem.at[r]
                    )
                    c.start()
                    stores.append(c)
                elif fresh_rows:
                    best_out[0][span, :] = top
                else:
                    best_out[part][span, :] = top
        for c in stores:
            c.wait()

    return kernel


def block_call(where, rows, cols, out, row_inv=None, col_inv=None, best=None, last=False):
    fresh_rows, fresh_cols = row_inv is None, col_inv is None
    n_rb = len(rows) if fresh_rows else 16
    n_cb = len(cols) if fresh_cols else cols[0].shape[0] // 128
    width = rows[0].shape[1]
    any_spec = pl.BlockSpec(memory_space=pl.ANY)
    vmem_spec = pl.BlockSpec(memory_space=pltpu.VMEM)
    args = [where, *rows, *cols]
    in_specs = [pl.BlockSpec(memory_space=pltpu.SMEM)]
    in_specs += [any_spec if fresh_rows else vmem_spec] * len(rows)
    in_specs += [any_spec if fresh_cols else vmem_spec] * len(cols)
    for extra in (row_inv, col_inv, best):
        if extra is not None:
            extra = extra if isinstance(extra, (list, tuple)) else [extra]
            args += extra
            in_specs += [vmem_spec] * len(extra)
    aliases = {}
    if out is not None:
        args.append(out)
        in_specs.append(vmem_spec)
        aliases = {len(args) - 1: 0}
    out_shape = [jax.ShapeDtypeStruct((2048, 1024), BF16)]
    if last:
        out_shape.append(jax.ShapeDtypeStruct((2048, 1024), BF16))
        out_shape.append(jax.ShapeDtypeStruct((16, 128), F32))
    else:
        out_shape += [jax.ShapeDtypeStruct((1024, 128), F32)] * (1 if fresh_rows else 2)
    if fresh_rows:
        out_shape.append(jax.ShapeDtypeStruct((128 * n_rb, width), BF16))
        out_shape.append(jax.ShapeDtypeStruct((128 * n_rb, 128), F32))
    if fresh_cols:
        out_shape.append(jax.ShapeDtypeStruct((128 * n_cb, width), BF16))
        out_shape.append(jax.ShapeDtypeStruct((8, 128 * n_cb), F32))
    return pl.pallas_call(
        make_block_kernel(n_rb, n_cb, fresh_rows, fresh_cols, out is None, last),
        out_shape=out_shape,
        in_specs=in_specs,
        out_specs=[any_spec if last and n == 1 else vmem_spec for n in range(len(out_shape))],
        input_output_aliases=aliases,
        scratch_shapes=[
            pltpu.SemaphoreType.DMA((n_rb,)),
            pltpu.SemaphoreType.DMA((n_cb,)),
            pltpu.SemaphoreType.DMA((n_rb,)),
        ],
        compiler_params=pltpu.CompilerParams(vmem_limit_bytes=VMEM_LIMIT),
        cost_estimate=pl.CostEstimate(
            flops=2 * n_rb * n_cb * 128 * 128 * width,
            bytes_accessed=2 * n_rb * n_cb * 128 * 128,
            transcendentals=0,
        ),
    )(*args)


VMEM_LIMIT = 12 * MIB


def tied(value, *others):
    return lax.optimization_barrier((value,) + others)[0]


def per_device(items, position_of):
    count, width = items.shape
    vmem_spec = pl.BlockSpec(memory_space=pltpu.VMEM)
    packed = pl.pallas_call(
        pack_kernel,
        out_shape=jax.ShapeDtypeStruct((count, width + 128), BF16),
        in_specs=[vmem_spec, vmem_spec],
        out_specs=vmem_spec,
    )(position_of.reshape(1, count), items)
    gr, gc = lax.axis_index("gr"), lax.axis_index("gc")
    yh, z = gr // 4, gr % 4
    x, yl, core = gc // 4, (gc // 2) % 2, gc % 2
    ring = 1 - 2 * core

    def row_at(dx=0, dy=0, dc=0):
        return ((x + dx + 4) % 4) * 4 + ((yl + dy) % 2) * 2 + (core + dc) % 2

    def col_at(dy=0, dz=0):
        return ((yh + dy) % 2) * 4 + (z + dz + 4) % 4

    rows_at_1 = [
        row_at(), row_at(dc=1), row_at(-ring), row_at(-ring, dc=1),
        row_at(ring, dc=1), row_at(ring), row_at(dy=1), row_at(dy=1, dc=1),
    ]
    rows_at_2 = [
        row_at(-ring, 1), row_at(-ring, 1, 1), row_at(ring, 1, 1), row_at(ring, 1),
        row_at(2), row_at(2, dc=1), row_at(2, 1), row_at(2, 1, 1),
    ]
    cols_at_1 = [col_at(), col_at(dz=-ring), col_at(dz=ring), col_at(dz=2)]
    cols_at_2 = [col_at(1, -ring), col_at(1, ring)]
    cols_at_3 = [col_at(1), col_at(1, 2)]
    places = jnp.stack(
        rows_at_1 + cols_at_1 + rows_at_2 + cols_at_1
        + rows_at_1 + rows_at_2 + cols_at_2
        + rows_at_1 + rows_at_2 + cols_at_3
    ).astype(jnp.int32)
    where_1, where_2, where_3, where_4 = (
        places[:12], places[12:24], places[24:42], places[42:60]
    )
    packed, where_1, where_2, where_3, where_4 = lax.optimization_barrier(
        (packed, where_1, where_2, where_3, where_4)
    )
    arrived = lax.all_to_all(packed, AXES, split_axis=0, concat_axis=0, tiled=True)
    own, own_low, own_high = pl.pallas_call(
        place_kernel,
        out_shape=[
            jax.ShapeDtypeStruct((count, width), BF16),
            jax.ShapeDtypeStruct((count // 2, width), BF16),
            jax.ShapeDtypeStruct((count // 2, width), BF16),
        ],
        in_specs=[vmem_spec],
        out_specs=[vmem_spec] * 3,
    )(arrived)

    cross, up_x, up_z = {"c": 1}, {"x": "ring"}, {"z": "ring"}
    pair_low = send(own_low, {"yl": 1})
    pair_high = send(tied(own_high, pair_low), {"yl": 1})
    far_low = send(pair_low, {"yh": 1, "yl": 1})
    far_high = send(pair_high, {"yh": 1, "yl": 1})
    pair, far = join(pair_low, pair_high), join(far_low, far_high)
    own_c = send(own, cross)
    x_a, z_a = send(own, up_x), send(own, up_z)
    x_b, z_b = send(own_c, up_x), send(own_c, up_z)
    x_2, z_2 = send(x_a, up_x), send(z_a, up_z)
    pair_c, x_a_c, x_b_c, z_b_c = (send(v, cross) for v in (pair, x_a, x_b, z_b))
    p_a, p_b = send(pair, up_x), send(pair_c, up_x)
    out, best_1, rows_1, inv_1, cols_1, col_inv_1 = block_call(
        tied(where_1, far),
        [own, own_c, x_a, x_b, x_a_c, x_b_c, pair, pair_c],
        [own, z_a, z_b_c, z_2],
        None,
    )
    far_c = send(far, cross)
    f_a, f_b = send(far, up_z), send(tied(far_c, best_1), up_z)
    p_2 = send(x_2, {"yl": 1})
    p_a_c, p_b_c, x_2_c, p_2_c = (send(v, cross) for v in (p_a, p_b, x_2, p_2))
    out, best_2, rows_2, inv_2 = block_call(
        where_2,
        [p_a, p_b, p_a_c, p_b_c, x_2, x_2_c, p_2, p_2_c],
        [cols_1],
        out,
        col_inv=col_inv_1,
    )
    f_b_c = send(f_b, cross)
    f_2 = send(f_a, up_z)
    out, best_1, best_2, _, _ = block_call(
        where_3, [rows_1, rows_2], [f_a, f_b_c], out, row_inv=[inv_1, inv_2], best=[best_1, best_2]
    )
    _, out, best, _, _ = block_call(
        where_4,
        [rows_1, rows_2],
        [far, f_2],
        out,
        row_inv=[inv_1, inv_2],
        best=[best_1, best_2],
        last=True,
    )

    best = jnp.maximum(best, send(best, cross))
    best = jnp.maximum(best, send(best, {"yl": 1}))
    best = jnp.maximum(
        jnp.maximum(best, send(best, {"x": 2})),
        jnp.maximum(send(best, {"x": 1}), send(best, {"x": -1})),
    )
    return out, best.reshape(-1)


def solution(mesh):
    return jax.shard_map(
        per_device,
        mesh=mesh,
        in_specs=(P(("gr", "gc"), None), P(("gr", "gc"))),
        out_specs=(P("gr", "gc"), P("gr")),
        check_vma=False,
    )
```

```python
import jax
import jax.numpy as jnp
from jax import lax
from jax.experimental import pallas as pl
from jax.experimental.pallas import tpu as pltpu
from jax.sharding import PartitionSpec as P

AXES = ("gr", "gc")
SIZES = {"yh": 2, "z": 4, "x": 4, "yl": 2, "c": 2}
F32 = jnp.float32
BF16 = jnp.bfloat16
MIB = 1024 * 1024


def coords(d):
    gr, gc = divmod(d, 16)
    return {"yh": gr // 4, "z": gr % 4, "x": gc // 4, "yl": (gc // 2) % 2, "c": gc % 2}


def flat(c):
    return (c["yh"] * 4 + c["z"]) * 16 + c["x"] * 4 + c["yl"] * 2 + c["c"]


def send(value, route):
    pairs = []
    for d in range(128):
        c = coords(d)
        for k, v in route.items():
            if v == "ring":
                v = 1 if c["c"] == 0 else -1
            elif v == "even":
                v = 1 if c[k] % 2 == 0 else -1
            elif v == "odd":
                v = 1 if c[k] % 2 == 1 else -1
            c[k] = (c[k] + v) % SIZES[k]
        pairs.append((d, flat(c)))
    return lax.ppermute(value, AXES, pairs)


def pack_kernel(pos_ref, items_ref, out_ref):
    count, width = items_ref.shape
    pos = pos_ref[...]
    dest = lax.broadcasted_iota(jnp.int32, (count, count), 0)
    hit = (pos // count) == dest
    pick = jnp.where(hit, 1.0, 0.0).astype(BF16)
    step = 1024
    for s in range(0, width, step):
        out_ref[:, s : s + step] = jnp.dot(
            pick, items_ref[:, s : s + step], preferred_element_type=F32
        ).astype(BF16)
    slot = jnp.sum(jnp.where(hit, (pos % count).astype(F32), 0.0), axis=1, keepdims=True)
    out_ref[:, width:] = jnp.broadcast_to(slot, (count, out_ref.shape[1] - width)).astype(BF16)


def place_kernel(in_ref, out_ref):
    count, width = out_ref.shape
    slot = in_ref[:, width : width + 128].astype(F32)
    lane = lax.broadcasted_iota(jnp.int32, (count, count), 1).astype(F32)
    pick = jnp.where(slot == lane, 1.0, 0.0).astype(BF16)
    step = 1024
    for s in range(0, width, step):
        out_ref[:, s : s + step] = lax.dot_general(
            pick, in_ref[:, s : s + step], (((0,), (0,)), ((), ())), preferred_element_type=F32
        ).astype(BF16)


def moved(sources, sizes):
    width = sources[0].shape[1]
    ins, at = [], 0
    for n, s in enumerate(sources):
        ins.append((n, at, at + s.shape[0]))
        at += s.shape[0]
    pieces, at = [], 0
    for m, size in enumerate(sizes):
        for n, lo, hi in ins:
            start, end = max(lo, at), min(hi, at + size)
            if start < end:
                pieces.append((n, start - lo, m, start - at, end - start))
        at += size

    def kernel(*refs):
        src, dst, sems = refs[: len(sources)], refs[len(sources) : -1], refs[-1]
        copies = [
            pltpu.make_async_copy(
                src[n].at[pl.ds(i, rows)], dst[m].at[pl.ds(o, rows)], sems.at[k]
            )
            for k, (n, i, m, o, rows) in enumerate(pieces)
        ]
        for c in copies:
            c.start()
        for c in copies:
            c.wait()

    return pl.pallas_call(
        kernel,
        out_shape=[jax.ShapeDtypeStruct((size, width), BF16) for size in sizes],
        in_specs=[pl.BlockSpec(memory_space=pl.ANY)] * len(sources),
        out_specs=[pl.BlockSpec(memory_space=pltpu.VMEM)] * len(sizes),
        scratch_shapes=[pltpu.SemaphoreType.DMA((len(pieces),))],
        compiler_params=pltpu.CompilerParams(vmem_limit_bytes=2 * MIB),
    )(*sources)


def pick_kernel(core_ref, up_ref, down_ref, out_ref, sem):
    def take(src):
        c = pltpu.make_async_copy(src, out_ref, sem)
        c.start()
        c.wait()

    @pl.when(core_ref[0] == 0)
    def _():
        take(up_ref)

    @pl.when(core_ref[0] != 0)
    def _():
        take(down_ref)


def pick(core, up, down):
    any_spec = pl.BlockSpec(memory_space=pl.ANY)
    return pl.pallas_call(
        pick_kernel,
        out_shape=jax.ShapeDtypeStruct(up.shape, BF16),
        in_specs=[pl.BlockSpec(memory_space=pltpu.SMEM), any_spec, any_spec],
        out_specs=pl.BlockSpec(memory_space=pltpu.VMEM),
        scratch_shapes=[pltpu.SemaphoreType.DMA],
        compiler_params=pltpu.CompilerParams(vmem_limit_bytes=2 * MIB),
    )(core, up, down)


def inverse_norm(ref, start, rows):
    total = jnp.zeros((rows, 128), F32)
    for s in range(0, ref.shape[1], 128):
        part = ref[start : start + rows, s : s + 128].astype(F32)
        total = total + part * part
    return 1.0 / jnp.sqrt(jnp.sum(total, axis=1, keepdims=True) + 1e-06)


def across(column):
    return jnp.transpose(jnp.broadcast_to(column, (128, 128)))[:1, :]


def make_block_kernel(row_sizes, col_sizes, fresh_rows, fresh_cols, diagonal, last):
    n_rb, n_cb = sum(row_sizes) // 128, sum(col_sizes) // 128
    tile = 512
    per_tile = tile // 128

    def kernel(*refs):
        refs = list(refs)

        def grab(count):
            return [refs.pop(0) for _ in range(count)]

        (where,) = grab(1)
        row_refs, col_refs = grab(len(row_sizes)), grab(len(col_sizes))
        row_inv = [] if fresh_rows else grab(len(row_sizes))
        col_inv = [] if fresh_cols else grab(len(col_sizes))
        best_in = [] if fresh_rows else grab(len(row_sizes))
        if not diagonal:
            grab(1)
        (out_ref,) = grab(1)
        best_out = grab(1 if fresh_rows or last else len(row_sizes))
        if fresh_rows:
            rows_v, row_inv_out = grab(2)
        if fresh_cols:
            cols_v, col_inv_out = grab(2)
        row_sem, col_sem = refs

        def loads(sources, sizes, target, sems):
            made, at = [], 0
            for n, (ref, size) in enumerate(zip(sources, sizes)):
                c = pltpu.make_async_copy(
                    ref.at[pl.ds(0, size)], target.at[pl.ds(at, size)], sems.at[n]
                )
                c.start()
                made.append((at, c))
                at += size
            return made

        col_loads = loads(col_refs, col_sizes, cols_v, col_sem) if fresh_cols else []
        row_loads = loads(row_refs, row_sizes, rows_v, row_sem) if fresh_rows else []
        for _, c in col_loads:
            c.wait()
        if fresh_cols:
            for lane in range(0, sum(col_sizes), 128):
                col_inv_out[:, lane : lane + 128] = jnp.broadcast_to(
                    across(inverse_norm(cols_v, lane, 128)), (8, 128)
                )
        if fresh_cols:
            groups = [(0, cols_v, col_inv_out)]
        else:
            starts = [sum(col_sizes[:n]) for n in range(len(col_sizes))]
            groups = list(zip(starts, col_refs, col_inv))
        for t in range(n_rb // per_tile):
            if fresh_rows:
                while row_loads and row_loads[0][0] < (t + 1) * tile:
                    row_loads.pop(0)[1].wait()
                source, part, base = rows_v, None, t * tile
            else:
                part, base = t, 0
                source = row_refs[part]
            products = [
                lax.dot_general(
                    source[base : base + tile, :],
                    ref[...],
                    (((1,), (1,)), ((), ())),
                    preferred_element_type=F32,
                )
                for _, ref, _ in groups
            ]
            for k in range(per_tile):
                r = t * per_tile + k
                span = slice(base + 128 * k, base + 128 * k + 128)
                if fresh_rows:
                    inv = jnp.broadcast_to(inverse_norm(rows_v, span.start, 128), (128, 128))
                    row_inv_out[span, :] = inv
                    top = None
                else:
                    inv = row_inv[part][span, :]
                    top = best_in[part][span, :]
                a = where[r]
                here = pl.ds(pl.multiple_of(a * 128, 128), 128)
                for (first, ref, inv_ref), product in zip(groups, products):
                    for lane in range(0, ref.shape[0], 128):
                        lanes = slice(lane, lane + 128)
                        scaled = product[128 * k : 128 * k + 128, lanes] * inv * inv_ref[:1, lanes]
                        there = where[n_rb + (first + lane) // 128]
                        out_ref[here, pl.ds(pl.multiple_of(there * 128, 128), 128)] = scaled.astype(
                            BF16
                        )
                        if diagonal and r == 0 and first + lane == 0:
                            across_i = lax.broadcasted_iota(jnp.int32, scaled.shape, 1)
                            down_i = lax.broadcasted_iota(jnp.int32, scaled.shape, 0)
                            scaled = jnp.where(across_i == down_i, -2.0, scaled)
                        top = scaled if top is None else jnp.maximum(top, scaled)
                if last:
                    best_out[0][pl.ds(a, 1), :] = across(jnp.max(top, axis=1, keepdims=True))
                elif fresh_rows:
                    best_out[0][span, :] = top
                else:
                    best_out[part][span, :] = top

    return kernel


def block_call(where, rows, cols, out, row_inv=None, col_inv=None, best=None, last=False):
    fresh_rows, fresh_cols = row_inv is None, col_inv is None
    row_sizes, col_sizes = [r.shape[0] for r in rows], [c.shape[0] for c in cols]
    n_rows, n_cols = sum(row_sizes), sum(col_sizes)
    width = rows[0].shape[1]
    any_spec = pl.BlockSpec(memory_space=pl.ANY)
    vmem_spec = pl.BlockSpec(memory_space=pltpu.VMEM)
    args = [where, *rows, *cols]
    in_specs = [pl.BlockSpec(memory_space=pltpu.SMEM)]
    in_specs += [any_spec if fresh_rows else vmem_spec] * len(rows)
    in_specs += [any_spec if fresh_cols else vmem_spec] * len(cols)
    for extra in (row_inv, col_inv, best):
        if extra is not None:
            args += extra
            in_specs += [vmem_spec] * len(extra)
    aliases = {}
    if out is not None:
        args.append(out)
        in_specs.append(vmem_spec)
        aliases = {len(args) - 1: 0}
    out_shape = [jax.ShapeDtypeStruct((2048, 1024), BF16)]
    if last:
        out_shape.append(jax.ShapeDtypeStruct((16, 128), F32))
    else:
        out_shape += [jax.ShapeDtypeStruct((512, 128), F32)] * (1 if fresh_rows else len(rows))
    if fresh_rows:
        out_shape.append(jax.ShapeDtypeStruct((n_rows, width), BF16))
        out_shape.append(jax.ShapeDtypeStruct((n_rows, 128), F32))
    if fresh_cols:
        out_shape.append(jax.ShapeDtypeStruct((n_cols, width), BF16))
        out_shape.append(jax.ShapeDtypeStruct((8, n_cols), F32))
    return pl.pallas_call(
        make_block_kernel(row_sizes, col_sizes, fresh_rows, fresh_cols, out is None, last),
        out_shape=out_shape,
        in_specs=in_specs,
        out_specs=[vmem_spec] * len(out_shape),
        input_output_aliases=aliases,
        scratch_shapes=[
            pltpu.SemaphoreType.DMA((len(rows),)),
            pltpu.SemaphoreType.DMA((len(cols),)),
        ],
        compiler_params=pltpu.CompilerParams(vmem_limit_bytes=VMEM_LIMIT),
        cost_estimate=pl.CostEstimate(
            flops=n_rows * n_cols * width // 4,
            bytes_accessed=2 * n_rows * n_cols,
            transcendentals=0,
        ),
    )(*args)


def store_kernel(held_ref, out_ref, sems):
    rows = held_ref.shape[0] // sems.shape[0]
    copies = [
        pltpu.make_async_copy(
            held_ref.at[pl.ds(rows * n, rows)], out_ref.at[pl.ds(rows * n, rows)], sems.at[n]
        )
        for n in range(sems.shape[0])
    ]
    for c in copies:
        c.start()
    for c in copies:
        c.wait()


def store(held):
    return pl.pallas_call(
        store_kernel,
        out_shape=jax.ShapeDtypeStruct(held.shape, held.dtype),
        in_specs=[pl.BlockSpec(memory_space=pltpu.VMEM)],
        out_specs=pl.BlockSpec(memory_space=pl.ANY),
        scratch_shapes=[pltpu.SemaphoreType.DMA((4,))],
        compiler_params=pltpu.CompilerParams(vmem_limit_bytes=2 * MIB),
        cost_estimate=pl.CostEstimate(
            flops=0, bytes_accessed=2 * held.size * 2, transcendentals=0
        ),
    )(held)


VMEM_LIMIT = 12 * MIB


def fence(*values):
    return lax.optimization_barrier(values)


def per_device(items, position_of):
    count, width = items.shape
    vmem_spec = pl.BlockSpec(memory_space=pltpu.VMEM)
    packed = pl.pallas_call(
        pack_kernel,
        out_shape=jax.ShapeDtypeStruct((count, width + 1024), BF16),
        in_specs=[vmem_spec, vmem_spec],
        out_specs=vmem_spec,
    )(position_of.reshape(1, count), items)
    gr, gc = lax.axis_index("gr"), lax.axis_index("gc")
    yh, z = gr // 4, gr % 4
    x, yl, core = gc // 4, (gc // 2) % 2, gc % 2

    def row_at(dx=0, dy=0, dc=0):
        return ((x + dx + 4) % 4) * 4 + ((yl + dy) % 2) * 2 + (core + dc) % 2

    def col_at(dy=0, dz=0):
        return ((yh + dy) % 2) * 4 + (z + dz + 4) % 4

    ring = 1 - 2 * core
    rows_at = [
        [row_at(), row_at(dc=1), row_at(-ring), row_at(-ring, dc=1)],
        [row_at(dy=1), row_at(dy=1, dc=1), row_at(ring, dc=1), row_at(ring)],
        [row_at(2), row_at(-ring, 1, 1), row_at(2, dc=1), row_at(ring, 1)],
        [row_at(-ring, 1), row_at(ring, 1, 1), row_at(2, 1), row_at(2, 1, 1)],
    ]
    cols_at = [
        [col_at(), col_at(dz=-ring)],
        [col_at(dz=ring), col_at(dz=2)],
        [col_at(1), col_at(1, -ring)],
        [col_at(1, ring), col_at(1, 2)],
    ]

    def places(rows, cols):
        flat_list = sum([rows_at[r] for r in rows], []) + sum([cols_at[c] for c in cols], [])
        return jnp.stack(flat_list).astype(jnp.int32)

    packed, *where = fence(
        packed,
        places([0], [0]),
        places([1], [0]),
        places([0, 1], [1]),
        places([2], [0, 1]),
        places([0, 1, 2], [2]),
        places([3], [0, 1, 2]),
        places([0, 1, 2, 3], [3]),
    )
    arrived = lax.all_to_all(
        packed.reshape(count, -1, 128), AXES, split_axis=0, concat_axis=0, tiled=True
    ).reshape(count, -1)
    own = pl.pallas_call(
        place_kernel,
        out_shape=jax.ShapeDtypeStruct((count, width), BF16),
        in_specs=[vmem_spec],
        out_specs=vmem_spec,
    )(arrived)

    cross, near, over = {"c": 1}, {"yl": 1}, {"yh": 1, "yl": 1}
    up_x, up_z = {"x": "ring"}, {"z": "ring"}
    def swap(value):
        return [send(v, cross) for v in moved([value], [count // 2] * 2)]

    own_c = send(own, cross)
    x_a, z_a, pair = send(own, up_x), send(own, up_z), send(own, near)
    x_b, z_b = send(own_c, up_x), send(own_c, up_z)
    pair_c = swap(pair)
    own_c, x_a, x_b, z_a, z_b, pair, *pair_c = fence(own_c, x_a, x_b, z_a, z_b, pair, *pair_c)

    (x_ring,) = moved([x_a, *pair_c], [256])
    x_2 = send(x_ring, up_x)
    p_a, far = send(x_a, near), send(pair, over)
    x_a_c, x_b_c = send(x_a, cross), send(x_b, cross)
    out, best_1, rows_1, inv_1, cols_1, col_inv_1 = block_call(
        where[0], [own, own_c, x_a, x_b], [own, z_a], None
    )
    out, best_2, rows_2, inv_2 = block_call(
        where[1], [pair, *pair_c, x_a_c, x_b_c], [cols_1], out, col_inv=[col_inv_1]
    )
    z_a, z_b, best_2 = fence(z_a, z_b, best_2)
    z_2, z_b_c = send(z_a, up_z), send(z_b, cross)
    far, p_a, z_b_c, x_2 = fence(far, p_a, z_b_c, x_2)
    far_c, p_a_c = swap(far), swap(p_a)
    (far_c,) = moved(far_c, [count])
    x_2, p_a, far, z_2, far_c, z_b_c, best_2, *p_a_c = fence(
        x_2, p_a, far, z_2, far_c, z_b_c, best_2, *p_a_c
    )

    f_a, f_2, p_2 = send(far, up_z), send(z_2, {"yh": 1}), send(p_a, up_x)
    x_2_c = send(x_2, cross)
    out, best_1, best_2, cols_2, col_inv_2 = block_call(
        where[2], [rows_1, rows_2], [z_b_c, z_2], out, row_inv=[inv_1, inv_2], best=[best_1, best_2]
    )
    out, best_3, rows_3, inv_3 = block_call(
        where[3], [x_2, x_2_c], [cols_1, cols_2], out, col_inv=[col_inv_1, col_inv_2]
    )
    far_c, best_3 = fence(far_c, best_3)
    f_b = send(far_c, up_z)
    p_2, best_3 = fence(p_2, best_3)
    p_2_c = swap(p_2)
    out, best_1, best_2, best_3, cols_3, col_inv_3 = block_call(
        where[4],
        [rows_1, rows_2, rows_3],
        [far, f_a],
        out,
        row_inv=[inv_1, inv_2, inv_3],
        best=[best_1, best_2, best_3],
    )
    out, best_4, rows_4, inv_4 = block_call(
        where[5],
        [p_a, *p_a_c, p_2, *p_2_c],
        [cols_1, cols_2, cols_3],
        out,
        col_inv=[col_inv_1, col_inv_2, col_inv_3],
    )
    f_b, f_2, best_4 = fence(f_b, f_2, best_4)
    f_b_c = swap(f_b)
    out, best, _, _ = block_call(
        where[6],
        [rows_1, rows_2, rows_3, rows_4],
        [*f_b_c, f_2],
        out,
        row_inv=[inv_1, inv_2, inv_3, inv_4],
        best=[best_1, best_2, best_3, best_4],
        last=True,
    )

    best = jnp.maximum(best, send(best, cross))
    best = jnp.maximum(best, send(best, near))
    best = jnp.maximum(best, send(best, {"x": "even"}))
    best, out = fence(best, store(out))
    best = jnp.maximum(best, send(best, {"x": "odd"}))
    return out, best.reshape(-1)


def solution(mesh):
    return jax.shard_map(
        per_device,
        mesh=mesh,
        in_specs=(P(("gr", "gc"), None), P(("gr", "gc"))),
        out_specs=(P("gr", "gc"), P("gr")),
        check_vma=False,
    )
```

```python
import jax
import jax.numpy as jnp
from jax import lax
from jax.experimental import pallas as pl
from jax.experimental.pallas import tpu as pltpu
from jax.sharding import PartitionSpec as P

AXES = ("gr", "gc")
SIZES = {"yh": 2, "z": 4, "x": 4, "yl": 2, "c": 2}
F32 = jnp.float32
BF16 = jnp.bfloat16
MIB = 1024 * 1024


def coords(d):
    gr, gc = divmod(d, 16)
    return {"yh": gr // 4, "z": gr % 4, "x": gc // 4, "yl": (gc // 2) % 2, "c": gc % 2}


def flat(c):
    return (c["yh"] * 4 + c["z"]) * 16 + c["x"] * 4 + c["yl"] * 2 + c["c"]


def send(value, route):
    pairs = []
    for d in range(128):
        c = coords(d)
        for k, v in route.items():
            if v == "ring":
                v = 1 if c["c"] == 0 else -1
            elif v == "even":
                v = 1 if c[k] % 2 == 0 else -1
            elif v == "odd":
                v = 1 if c[k] % 2 == 1 else -1
            c[k] = (c[k] + v) % SIZES[k]
        pairs.append((d, flat(c)))
    return lax.ppermute(value, AXES, pairs)


def pack_kernel(pos_ref, items_ref, out_ref):
    count, width = items_ref.shape
    pos = pos_ref[...]
    dest = lax.broadcasted_iota(jnp.int32, (count, count), 0)
    hit = (pos // count) == dest
    pick = jnp.where(hit, 1.0, 0.0).astype(BF16)
    step = 1024
    for s in range(0, width, step):
        part = jnp.dot(pick, items_ref[:, s : s + step], preferred_element_type=F32)
        out_ref[:, s // 128 : (s + step) // 128, :] = part.reshape(count, 8, 128).astype(BF16)
    slot = jnp.sum(jnp.where(hit, (pos % count).astype(F32), 0.0), axis=1, keepdims=True)
    out_ref[:, width // 128 :, :] = jnp.broadcast_to(slot[:, :, None], (count, 8, 128)).astype(BF16)


def place_kernel(in_ref, out_ref):
    count, width = out_ref.shape
    slot = in_ref[:, width // 128, :].astype(F32)
    lane = lax.broadcasted_iota(jnp.int32, (count, count), 1).astype(F32)
    pick = jnp.where(slot == lane, 1.0, 0.0).astype(BF16)
    step = 1024
    for s in range(0, width, step):
        part = in_ref[:, s // 128 : (s + step) // 128, :].astype(F32).reshape(count, step)
        out_ref[:, s : s + step] = lax.dot_general(
            pick, part.astype(BF16), (((0,), (0,)), ((), ())), preferred_element_type=F32
        ).astype(BF16)


def moved(sources, sizes):
    width = sources[0].shape[1]
    ins, at = [], 0
    for n, s in enumerate(sources):
        ins.append((n, at, at + s.shape[0]))
        at += s.shape[0]
    pieces, at = [], 0
    for m, size in enumerate(sizes):
        for n, lo, hi in ins:
            start, end = max(lo, at), min(hi, at + size)
            if start < end:
                pieces.append((n, start - lo, m, start - at, end - start))
        at += size

    def kernel(*refs):
        src, dst, sems = refs[: len(sources)], refs[len(sources) : -1], refs[-1]
        copies = [
            pltpu.make_async_copy(
                src[n].at[pl.ds(i, rows)], dst[m].at[pl.ds(o, rows)], sems.at[k]
            )
            for k, (n, i, m, o, rows) in enumerate(pieces)
        ]
        for c in copies:
            c.start()
        for c in copies:
            c.wait()

    return pl.pallas_call(
        kernel,
        out_shape=[jax.ShapeDtypeStruct((size, width), BF16) for size in sizes],
        in_specs=[pl.BlockSpec(memory_space=pl.ANY)] * len(sources),
        out_specs=[pl.BlockSpec(memory_space=pltpu.VMEM)] * len(sizes),
        scratch_shapes=[pltpu.SemaphoreType.DMA((len(pieces),))],
        compiler_params=pltpu.CompilerParams(vmem_limit_bytes=2 * MIB),
    )(*sources)


def pick_kernel(core_ref, up_ref, down_ref, out_ref, sem):
    def take(src):
        c = pltpu.make_async_copy(src, out_ref, sem)
        c.start()
        c.wait()

    @pl.when(core_ref[0] == 0)
    def _():
        take(up_ref)

    @pl.when(core_ref[0] != 0)
    def _():
        take(down_ref)


def pick(core, up, down):
    any_spec = pl.BlockSpec(memory_space=pl.ANY)
    return pl.pallas_call(
        pick_kernel,
        out_shape=jax.ShapeDtypeStruct(up.shape, BF16),
        in_specs=[pl.BlockSpec(memory_space=pltpu.SMEM), any_spec, any_spec],
        out_specs=pl.BlockSpec(memory_space=pltpu.VMEM),
        scratch_shapes=[pltpu.SemaphoreType.DMA],
        compiler_params=pltpu.CompilerParams(vmem_limit_bytes=2 * MIB),
    )(core, up, down)


def inverse_norm(ref, start, rows):
    total = jnp.zeros((rows, 128), F32)
    for s in range(0, ref.shape[1], 128):
        part = ref[start : start + rows, s : s + 128].astype(F32)
        total = total + part * part
    return 1.0 / jnp.sqrt(jnp.sum(total, axis=1, keepdims=True) + 1e-06)


def across(column):
    return jnp.transpose(jnp.broadcast_to(column, (128, 128)))[:1, :]


def make_block_kernel(line, row_sizes, col_sizes, fresh_rows, fresh_cols, diagonal, last):
    n_rb, n_cb = sum(row_sizes) // 128, sum(col_sizes) // 128
    tile = 512
    per_tile = tile // 128

    def kernel(*refs):
        refs = list(refs)

        def grab(count):
            return [refs.pop(0) for _ in range(count)]

        (where,) = grab(1)
        row_refs, col_refs = grab(len(row_sizes)), grab(len(col_sizes))
        row_inv = [] if fresh_rows else grab(len(row_sizes))
        col_inv = [] if fresh_cols else grab(len(col_sizes))
        best_in = [] if fresh_rows else grab(len(row_sizes))
        if not diagonal:
            grab(1)
        (out_ref,) = grab(1)
        best_out = grab(1 if fresh_rows or last else len(row_sizes))
        if fresh_rows:
            rows_v, row_inv_out = grab(2)
        if fresh_cols:
            cols_v, col_inv_out = grab(2)
        row_sem, col_sem = refs

        def loads(sources, sizes, target, sems):
            made, at = [], 0
            for n, (ref, size) in enumerate(zip(sources, sizes)):
                c = pltpu.make_async_copy(
                    ref.at[pl.ds(0, size)], target.at[pl.ds(at, size)], sems.at[n]
                )
                c.start()
                made.append((at, c))
                at += size
            return made

        col_loads = loads(col_refs, col_sizes, cols_v, col_sem) if fresh_cols else []
        row_loads = loads(row_refs, row_sizes, rows_v, row_sem) if fresh_rows else []
        for _, c in col_loads:
            c.wait()
        if fresh_cols:
            for lane in range(0, sum(col_sizes), 128):
                col_inv_out[:, lane : lane + 128] = jnp.broadcast_to(
                    across(inverse_norm(cols_v, lane, 128)), (8, 128)
                )
        if fresh_cols:
            groups = [(0, cols_v, col_inv_out)]
        else:
            starts = [sum(col_sizes[:n]) for n in range(len(col_sizes))]
            groups = list(zip(starts, col_refs, col_inv))
        for t in range(n_rb // per_tile):
            if fresh_rows:
                while row_loads and row_loads[0][0] < (t + 1) * tile:
                    row_loads.pop(0)[1].wait()
                source, part, base = rows_v, None, t * tile
            else:
                part, base = t, 0
                source = row_refs[part]
            products = [
                lax.dot_general(
                    source[base : base + tile, :],
                    ref[...],
                    (((1,), (1,)), ((), ())),
                    preferred_element_type=F32,
                )
                for _, ref, _ in groups
            ]
            for k in range(per_tile):
                r = t * per_tile + k
                span = slice(base + 128 * k, base + 128 * k + 128)
                if fresh_rows:
                    inv = jnp.broadcast_to(inverse_norm(rows_v, span.start, 128), (128, 128))
                    row_inv_out[span, :] = inv
                    top = None
                else:
                    inv = row_inv[part][span, :]
                    top = best_in[part][span, :]
                a = where[line, r]
                here = pl.ds(pl.multiple_of(a * 128, 128), 128)
                for (first, ref, inv_ref), product in zip(groups, products):
                    for lane in range(0, ref.shape[0], 128):
                        lanes = slice(lane, lane + 128)
                        scaled = product[128 * k : 128 * k + 128, lanes] * inv * inv_ref[:1, lanes]
                        there = where[line, n_rb + (first + lane) // 128]
                        out_ref[here, pl.ds(pl.multiple_of(there * 128, 128), 128)] = scaled.astype(
                            BF16
                        )
                        if diagonal and r == 0 and first + lane == 0:
                            across_i = lax.broadcasted_iota(jnp.int32, scaled.shape, 1)
                            down_i = lax.broadcasted_iota(jnp.int32, scaled.shape, 0)
                            scaled = jnp.where(across_i == down_i, -2.0, scaled)
                        top = scaled if top is None else jnp.maximum(top, scaled)
                if last:
                    best_out[0][pl.ds(a, 1), :] = across(jnp.max(top, axis=1, keepdims=True))
                elif fresh_rows:
                    best_out[0][span, :] = top
                else:
                    best_out[part][span, :] = top

    return kernel


def block_call(where, rows, cols, out, row_inv=None, col_inv=None, best=None, last=False):
    where, line = where
    fresh_rows, fresh_cols = row_inv is None, col_inv is None
    row_sizes, col_sizes = [r.shape[0] for r in rows], [c.shape[0] for c in cols]
    n_rows, n_cols = sum(row_sizes), sum(col_sizes)
    width = rows[0].shape[1]
    any_spec = pl.BlockSpec(memory_space=pl.ANY)
    vmem_spec = pl.BlockSpec(memory_space=pltpu.VMEM)
    args = [where, *rows, *cols]
    in_specs = [pl.BlockSpec(memory_space=pltpu.SMEM)]
    in_specs += [any_spec if fresh_rows else vmem_spec] * len(rows)
    in_specs += [any_spec if fresh_cols else vmem_spec] * len(cols)
    for extra in (row_inv, col_inv, best):
        if extra is not None:
            args += extra
            in_specs += [vmem_spec] * len(extra)
    aliases = {}
    if out is not None:
        args.append(out)
        in_specs.append(vmem_spec)
        aliases = {len(args) - 1: 0}
    out_shape = [jax.ShapeDtypeStruct((2048, 1024), BF16)]
    if last:
        out_shape.append(jax.ShapeDtypeStruct((16, 128), F32))
    else:
        out_shape += [jax.ShapeDtypeStruct((512, 128), F32)] * (1 if fresh_rows else len(rows))
    if fresh_rows:
        out_shape.append(jax.ShapeDtypeStruct((n_rows, width), BF16))
        out_shape.append(jax.ShapeDtypeStruct((n_rows, 128), F32))
    if fresh_cols:
        out_shape.append(jax.ShapeDtypeStruct((n_cols, width), BF16))
        out_shape.append(jax.ShapeDtypeStruct((8, n_cols), F32))
    return pl.pallas_call(
        make_block_kernel(line, row_sizes, col_sizes, fresh_rows, fresh_cols, out is None, last),
        out_shape=out_shape,
        in_specs=in_specs,
        out_specs=[vmem_spec] * len(out_shape),
        input_output_aliases=aliases,
        scratch_shapes=[
            pltpu.SemaphoreType.DMA((len(rows),)),
            pltpu.SemaphoreType.DMA((len(cols),)),
        ],
        compiler_params=pltpu.CompilerParams(vmem_limit_bytes=VMEM_LIMIT),
        cost_estimate=pl.CostEstimate(
            flops=n_rows * n_cols * width // 4,
            bytes_accessed=2 * n_rows * n_cols,
            transcendentals=0,
        ),
    )(*args)


def store_kernel(held_ref, out_ref, sems):
    rows = held_ref.shape[0] // sems.shape[0]
    copies = [
        pltpu.make_async_copy(
            held_ref.at[pl.ds(rows * n, rows)], out_ref.at[pl.ds(rows * n, rows)], sems.at[n]
        )
        for n in range(sems.shape[0])
    ]
    for c in copies:
        c.start()
    for c in copies:
        c.wait()


def store(held):
    return pl.pallas_call(
        store_kernel,
        out_shape=jax.ShapeDtypeStruct(held.shape, held.dtype),
        in_specs=[pl.BlockSpec(memory_space=pltpu.VMEM)],
        out_specs=pl.BlockSpec(memory_space=pl.ANY),
        scratch_shapes=[pltpu.SemaphoreType.DMA((4,))],
        compiler_params=pltpu.CompilerParams(vmem_limit_bytes=2 * MIB),
        cost_estimate=pl.CostEstimate(
            flops=0, bytes_accessed=2 * held.size * 2, transcendentals=0
        ),
    )(held)


VMEM_LIMIT = 12 * MIB


def fence(*values):
    return lax.optimization_barrier(values)


def per_device(items, position_of):
    count, width = items.shape
    vmem_spec = pl.BlockSpec(memory_space=pltpu.VMEM)
    packed = pl.pallas_call(
        pack_kernel,
        out_shape=jax.ShapeDtypeStruct((count, width // 128 + 8, 128), BF16),
        in_specs=[vmem_spec, vmem_spec],
        out_specs=vmem_spec,
    )(position_of.reshape(1, count), items)
    gr, gc = lax.axis_index("gr"), lax.axis_index("gc")
    yh, z = gr // 4, gr % 4
    x, yl, core = gc // 4, (gc // 2) % 2, gc % 2

    def row_at(dx=0, dy=0, dc=0):
        return ((x + dx + 4) % 4) * 4 + ((yl + dy) % 2) * 2 + (core + dc) % 2

    def col_at(dy=0, dz=0):
        return ((yh + dy) % 2) * 4 + (z + dz + 4) % 4

    ring = 1 - 2 * core
    rows_at = [
        [row_at(), row_at(dc=1), row_at(-ring), row_at(-ring, dc=1)],
        [row_at(dy=1), row_at(dy=1, dc=1), row_at(ring, dc=1), row_at(ring)],
        [row_at(2), row_at(-ring, 1, 1), row_at(2, dc=1), row_at(ring, 1)],
        [row_at(-ring, 1), row_at(ring, 1, 1), row_at(2, 1), row_at(2, 1, 1)],
    ]
    cols_at = [
        [col_at(), col_at(dz=-ring)],
        [col_at(dz=ring), col_at(dz=2)],
        [col_at(1), col_at(1, -ring)],
        [col_at(1, ring), col_at(1, 2)],
    ]

    def places(rows, cols):
        flat_list = sum([rows_at[r] for r in rows], []) + sum([cols_at[c] for c in cols], [])
        return flat_list

    lists = [
        places([0], [0]),
        places([1], [0]),
        places([0, 1], [1]),
        places([2], [0, 1]),
        places([0, 1, 2], [2]),
        places([3], [0, 1, 2]),
        places([0, 1, 2, 3], [3]),
    ]
    table = jnp.stack([jnp.stack(p + [p[0]] * (18 - len(p))) for p in lists]).astype(jnp.int32)
    packed, table = fence(packed, table)
    where = [(table, n) for n in range(len(lists))]
    arrived = lax.all_to_all(
        packed, AXES, split_axis=0, concat_axis=0, tiled=True
    )
    own = pl.pallas_call(
        place_kernel,
        out_shape=jax.ShapeDtypeStruct((count, width), BF16),
        in_specs=[vmem_spec],
        out_specs=vmem_spec,
    )(arrived)

    cross, near, over = {"c": 1}, {"yl": 1}, {"yh": 1, "yl": 1}
    up_x, up_z = {"x": "ring"}, {"z": "ring"}
    def swap(value):
        return [send(v, cross) for v in moved([value], [count // 2] * 2)]

    own_c = send(own, cross)
    x_a, z_a, pair = send(own, up_x), send(own, up_z), send(own, near)
    x_b, z_b = send(own_c, up_x), send(own_c, up_z)
    pair_c = swap(pair)
    own_c, x_a, x_b, z_a, z_b, pair, *pair_c = fence(own_c, x_a, x_b, z_a, z_b, pair, *pair_c)

    (x_ring,) = moved([x_a, *pair_c], [256])
    x_2 = send(x_ring, up_x)
    p_a, far = send(x_a, near), send(pair, over)
    x_a_c, x_b_c = send(x_a, cross), send(x_b, cross)
    out, best_1, rows_1, inv_1, cols_1, col_inv_1 = block_call(
        where[0], [own, own_c, x_a, x_b], [own, z_a], None
    )
    out, best_2, rows_2, inv_2 = block_call(
        where[1], [pair, *pair_c, x_a_c, x_b_c], [cols_1], out, col_inv=[col_inv_1]
    )
    z_a, z_b, best_2 = fence(z_a, z_b, best_2)
    z_2, z_b_c = send(z_a, up_z), send(z_b, cross)
    far, p_a, z_b_c, x_2 = fence(far, p_a, z_b_c, x_2)
    far_c = swap(far)
    (far_c,) = moved(far_c, [count])
    x_2, p_a, far, z_2, far_c, z_b_c, best_2 = fence(x_2, p_a, far, z_2, far_c, z_b_c, best_2)

    f_a, f_2, p_2 = send(far, up_z), send(z_2, {"yh": 1}), send(p_a, up_x)
    x_2_c, p_a_c = fence(send(x_2, cross), send(p_a, cross))
    out, best_1, best_2, cols_2, col_inv_2 = block_call(
        where[2], [rows_1, rows_2], [z_b_c, z_2], out, row_inv=[inv_1, inv_2], best=[best_1, best_2]
    )
    out, best_3, rows_3, inv_3 = block_call(
        where[3], [x_2, x_2_c], [cols_1, cols_2], out, col_inv=[col_inv_1, col_inv_2]
    )
    far_c, best_3 = fence(far_c, best_3)
    f_b = send(far_c, up_z)
    p_2, best_3 = fence(p_2, best_3)
    p_2_c = swap(p_2)
    out, best_1, best_2, best_3, cols_3, col_inv_3 = block_call(
        where[4],
        [rows_1, rows_2, rows_3],
        [far, f_a],
        out,
        row_inv=[inv_1, inv_2, inv_3],
        best=[best_1, best_2, best_3],
    )
    out, best_4, rows_4, inv_4 = block_call(
        where[5],
        [p_a, p_a_c, p_2, *p_2_c],
        [cols_1, cols_2, cols_3],
        out,
        col_inv=[col_inv_1, col_inv_2, col_inv_3],
    )
    f_b, f_2, best_4 = fence(f_b, f_2, best_4)
    f_b_c = swap(f_b)
    out, best, _, _ = block_call(
        where[6],
        [rows_1, rows_2, rows_3, rows_4],
        [*f_b_c, f_2],
        out,
        row_inv=[inv_1, inv_2, inv_3, inv_4],
        best=[best_1, best_2, best_3, best_4],
        last=True,
    )

    best = jnp.maximum(best, send(best, cross))
    others = [send(best, way) for way in (near, {"x": "even"}, {"yl": 1, "x": "even"})]
    best = jnp.maximum(jnp.maximum(best, others[0]), jnp.maximum(others[1], others[2]))
    best, out = fence(best, store(out))
    best = jnp.maximum(best, send(best, {"x": "odd"}))
    return out, best.reshape(-1)


def solution(mesh):
    return jax.shard_map(
        per_device,
        mesh=mesh,
        in_specs=(P(("gr", "gc"), None), P(("gr", "gc"))),
        out_specs=(P("gr", "gc"), P("gr")),
        check_vma=False,
    )
```

```python
import jax
import jax.numpy as jnp
from jax import lax
from jax.experimental import pallas as pl
from jax.experimental.pallas import tpu as pltpu
from jax.sharding import PartitionSpec as P

AXES = ("gr", "gc")
SIZES = {"yh": 2, "z": 4, "x": 4, "yl": 2, "c": 2}
F32 = jnp.float32
BF16 = jnp.bfloat16
MIB = 1024 * 1024


def coords(d):
    gr, gc = divmod(d, 16)
    return {"yh": gr // 4, "z": gr % 4, "x": gc // 4, "yl": (gc // 2) % 2, "c": gc % 2}


def flat(c):
    return (c["yh"] * 4 + c["z"]) * 16 + c["x"] * 4 + c["yl"] * 2 + c["c"]


def send(value, route):
    pairs = []
    for d in range(128):
        c = coords(d)
        for k, v in route.items():
            if v == "ring":
                v = 1 if c["c"] == 0 else -1
            elif v == "back":
                v = -1 if c["c"] == 0 else 1
            elif v == "even":
                v = 1 if c[k] % 2 == 0 else -1
            elif v == "odd":
                v = 1 if c[k] % 2 == 1 else -1
            c[k] = (c[k] + v) % SIZES[k]
        pairs.append((d, flat(c)))
    return lax.ppermute(value, AXES, pairs)


def pack_kernel(pos_ref, items_ref, out_ref):
    count, width = items_ref.shape
    pos = pos_ref[...]
    dest = lax.broadcasted_iota(jnp.int32, (count, count), 0)
    hit = (pos // count) == dest
    pick = jnp.where(hit, 1.0, 0.0).astype(BF16)
    step = 1024
    for s in range(0, width, step):
        part = jnp.dot(pick, items_ref[:, s : s + step], preferred_element_type=F32)
        out_ref[:, s // 128 : (s + step) // 128, :] = part.reshape(count, 8, 128).astype(BF16)
    slot = jnp.sum(jnp.where(hit, (pos % count).astype(F32), 0.0), axis=1, keepdims=True)
    out_ref[:, width // 128 :, :] = jnp.broadcast_to(slot[:, :, None], (count, 8, 128)).astype(BF16)


def place_kernel(in_ref, out_ref):
    count, width = out_ref.shape
    slot = in_ref[:, width // 128, :].astype(F32)
    lane = lax.broadcasted_iota(jnp.int32, (count, count), 1).astype(F32)
    pick = jnp.where(slot == lane, 1.0, 0.0).astype(BF16)
    step = 1024
    for s in range(0, width, step):
        part = in_ref[:, s // 128 : (s + step) // 128, :].astype(F32).reshape(count, step)
        out_ref[:, s : s + step] = lax.dot_general(
            pick, part.astype(BF16), (((0,), (0,)), ((), ())), preferred_element_type=F32
        ).astype(BF16)


def moved(sources, sizes):
    width = sources[0].shape[1]
    ins, at = [], 0
    for n, s in enumerate(sources):
        ins.append((n, at, at + s.shape[0]))
        at += s.shape[0]
    pieces, at = [], 0
    for m, size in enumerate(sizes):
        for n, lo, hi in ins:
            start, end = max(lo, at), min(hi, at + size)
            if start < end:
                pieces.append((n, start - lo, m, start - at, end - start))
        at += size

    def kernel(*refs):
        src, dst, sems = refs[: len(sources)], refs[len(sources) : -1], refs[-1]
        copies = [
            pltpu.make_async_copy(
                src[n].at[pl.ds(i, rows)], dst[m].at[pl.ds(o, rows)], sems.at[k]
            )
            for k, (n, i, m, o, rows) in enumerate(pieces)
        ]
        for c in copies:
            c.start()
        for c in copies:
            c.wait()

    return pl.pallas_call(
        kernel,
        out_shape=[jax.ShapeDtypeStruct((size, width), BF16) for size in sizes],
        in_specs=[pl.BlockSpec(memory_space=pl.ANY)] * len(sources),
        out_specs=[pl.BlockSpec(memory_space=pltpu.VMEM)] * len(sizes),
        scratch_shapes=[pltpu.SemaphoreType.DMA((len(pieces),))],
        compiler_params=pltpu.CompilerParams(vmem_limit_bytes=2 * MIB),
    )(*sources)


def pick_kernel(core_ref, up_ref, down_ref, out_ref, sem):
    def take(src):
        c = pltpu.make_async_copy(src, out_ref, sem)
        c.start()
        c.wait()

    @pl.when(core_ref[0] == 0)
    def _():
        take(up_ref)

    @pl.when(core_ref[0] != 0)
    def _():
        take(down_ref)


def pick(core, up, down):
    any_spec = pl.BlockSpec(memory_space=pl.ANY)
    return pl.pallas_call(
        pick_kernel,
        out_shape=jax.ShapeDtypeStruct(up.shape, BF16),
        in_specs=[pl.BlockSpec(memory_space=pltpu.SMEM), any_spec, any_spec],
        out_specs=pl.BlockSpec(memory_space=pltpu.VMEM),
        scratch_shapes=[pltpu.SemaphoreType.DMA],
        compiler_params=pltpu.CompilerParams(vmem_limit_bytes=2 * MIB),
    )(core, up, down)


def inverse_norm(ref, start, rows):
    total = jnp.zeros((rows, 128), F32)
    for s in range(0, ref.shape[1], 128):
        part = ref[start : start + rows, s : s + 128].astype(F32)
        total = total + part * part
    return 1.0 / jnp.sqrt(jnp.sum(total, axis=1, keepdims=True) + 1e-06)


def across(column):
    return jnp.transpose(jnp.broadcast_to(column, (128, 128)))[:1, :]


def make_block_kernel(line, row_sizes, col_sizes, fresh_rows, fresh_cols, diagonal, last):
    n_rb, n_cb = sum(row_sizes) // 128, sum(col_sizes) // 128
    tile = 512
    per_tile = tile // 128

    def kernel(*refs):
        refs = list(refs)

        def grab(count):
            return [refs.pop(0) for _ in range(count)]

        (where,) = grab(1)
        row_refs, col_refs = grab(len(row_sizes)), grab(len(col_sizes))
        row_inv = [] if fresh_rows else grab(len(row_sizes))
        col_inv = [] if fresh_cols else grab(len(col_sizes))
        best_in = [] if fresh_rows else grab(len(row_sizes))
        if not diagonal:
            grab(1)
        (out_ref,) = grab(1)
        best_out = grab(1 if fresh_rows or last else len(row_sizes))
        if fresh_rows:
            rows_v, row_inv_out = grab(2)
        if fresh_cols:
            cols_v, col_inv_out = grab(2)
        row_sem, col_sem = refs

        def loads(sources, sizes, target, sems):
            made, at = [], 0
            for n, (ref, size) in enumerate(zip(sources, sizes)):
                c = pltpu.make_async_copy(
                    ref.at[pl.ds(0, size)], target.at[pl.ds(at, size)], sems.at[n]
                )
                c.start()
                made.append((at, c))
                at += size
            return made

        col_loads = loads(col_refs, col_sizes, cols_v, col_sem) if fresh_cols else []
        row_loads = loads(row_refs, row_sizes, rows_v, row_sem) if fresh_rows else []
        for _, c in col_loads:
            c.wait()
        if fresh_cols:
            for lane in range(0, sum(col_sizes), 128):
                col_inv_out[:, lane : lane + 128] = jnp.broadcast_to(
                    across(inverse_norm(cols_v, lane, 128)), (8, 128)
                )
        if fresh_cols:
            groups = [(0, cols_v, col_inv_out)]
        else:
            starts = [sum(col_sizes[:n]) for n in range(len(col_sizes))]
            groups = list(zip(starts, col_refs, col_inv))
        for t in range(n_rb // per_tile):
            if fresh_rows:
                while row_loads and row_loads[0][0] < (t + 1) * tile:
                    row_loads.pop(0)[1].wait()
                source, part, base = rows_v, None, t * tile
            else:
                part, base = t, 0
                source = row_refs[part]
            products = [
                lax.dot_general(
                    source[base : base + tile, :],
                    ref[...],
                    (((1,), (1,)), ((), ())),
                    preferred_element_type=F32,
                )
                for _, ref, _ in groups
            ]
            for k in range(per_tile):
                r = t * per_tile + k
                span = slice(base + 128 * k, base + 128 * k + 128)
                if fresh_rows:
                    inv = jnp.broadcast_to(inverse_norm(rows_v, span.start, 128), (128, 128))
                    row_inv_out[span, :] = inv
                    top = None
                else:
                    inv = row_inv[part][span, :]
                    top = best_in[part][span, :]
                a = where[line, r]
                here = pl.ds(pl.multiple_of(a * 128, 128), 128)
                for (first, ref, inv_ref), product in zip(groups, products):
                    for lane in range(0, ref.shape[0], 128):
                        lanes = slice(lane, lane + 128)
                        scaled = product[128 * k : 128 * k + 128, lanes] * inv * inv_ref[:1, lanes]
                        there = where[line, n_rb + (first + lane) // 128]
                        out_ref[here, pl.ds(pl.multiple_of(there * 128, 128), 128)] = scaled.astype(
                            BF16
                        )
                        if diagonal and r == 0 and first + lane == 0:
                            across_i = lax.broadcasted_iota(jnp.int32, scaled.shape, 1)
                            down_i = lax.broadcasted_iota(jnp.int32, scaled.shape, 0)
                            scaled = jnp.where(across_i == down_i, -2.0, scaled)
                        top = scaled if top is None else jnp.maximum(top, scaled)
                if last:
                    best_out[0][pl.ds(a, 1), :] = across(jnp.max(top, axis=1, keepdims=True))
                elif fresh_rows:
                    best_out[0][span, :] = top
                else:
                    best_out[part][span, :] = top

    return kernel


def block_call(where, rows, cols, out, row_inv=None, col_inv=None, best=None, last=False):
    where, line = where
    fresh_rows, fresh_cols = row_inv is None, col_inv is None
    row_sizes, col_sizes = [r.shape[0] for r in rows], [c.shape[0] for c in cols]
    n_rows, n_cols = sum(row_sizes), sum(col_sizes)
    width = rows[0].shape[1]
    any_spec = pl.BlockSpec(memory_space=pl.ANY)
    vmem_spec = pl.BlockSpec(memory_space=pltpu.VMEM)
    args = [where, *rows, *cols]
    in_specs = [pl.BlockSpec(memory_space=pltpu.SMEM)]
    in_specs += [any_spec if fresh_rows else vmem_spec] * len(rows)
    in_specs += [any_spec if fresh_cols else vmem_spec] * len(cols)
    for extra in (row_inv, col_inv, best):
        if extra is not None:
            args += extra
            in_specs += [vmem_spec] * len(extra)
    aliases = {}
    if out is not None:
        args.append(out)
        in_specs.append(vmem_spec)
        aliases = {len(args) - 1: 0}
    out_shape = [jax.ShapeDtypeStruct((2048, 1024), BF16)]
    if last:
        out_shape.append(jax.ShapeDtypeStruct((16, 128), F32))
    else:
        out_shape += [jax.ShapeDtypeStruct((512, 128), F32)] * (1 if fresh_rows else len(rows))
    if fresh_rows:
        out_shape.append(jax.ShapeDtypeStruct((n_rows, width), BF16))
        out_shape.append(jax.ShapeDtypeStruct((n_rows, 128), F32))
    if fresh_cols:
        out_shape.append(jax.ShapeDtypeStruct((n_cols, width), BF16))
        out_shape.append(jax.ShapeDtypeStruct((8, n_cols), F32))
    return pl.pallas_call(
        make_block_kernel(line, row_sizes, col_sizes, fresh_rows, fresh_cols, out is None, last),
        out_shape=out_shape,
        in_specs=in_specs,
        out_specs=[vmem_spec] * len(out_shape),
        input_output_aliases=aliases,
        scratch_shapes=[
            pltpu.SemaphoreType.DMA((len(rows),)),
            pltpu.SemaphoreType.DMA((len(cols),)),
        ],
        compiler_params=pltpu.CompilerParams(vmem_limit_bytes=VMEM_LIMIT),
        cost_estimate=pl.CostEstimate(
            flops=n_rows * n_cols * width // 4,
            bytes_accessed=2 * n_rows * n_cols,
            transcendentals=0,
        ),
    )(*args)


def store_kernel(held_ref, out_ref, sems):
    rows = held_ref.shape[0] // sems.shape[0]
    copies = [
        pltpu.make_async_copy(
            held_ref.at[pl.ds(rows * n, rows)], out_ref.at[pl.ds(rows * n, rows)], sems.at[n]
        )
        for n in range(sems.shape[0])
    ]
    for c in copies:
        c.start()
    for c in copies:
        c.wait()


def store(held):
    return pl.pallas_call(
        store_kernel,
        out_shape=jax.ShapeDtypeStruct(held.shape, held.dtype),
        in_specs=[pl.BlockSpec(memory_space=pltpu.VMEM)],
        out_specs=pl.BlockSpec(memory_space=pl.ANY),
        scratch_shapes=[pltpu.SemaphoreType.DMA((4,))],
        compiler_params=pltpu.CompilerParams(vmem_limit_bytes=2 * MIB),
        cost_estimate=pl.CostEstimate(
            flops=0, bytes_accessed=2 * held.size * 2, transcendentals=0
        ),
    )(held)


VMEM_LIMIT = 12 * MIB


def fence(*values):
    return lax.optimization_barrier(values)


def per_device(items, position_of):
    count, width = items.shape
    vmem_spec = pl.BlockSpec(memory_space=pltpu.VMEM)
    packed = pl.pallas_call(
        pack_kernel,
        out_shape=jax.ShapeDtypeStruct((count, width // 128 + 8, 128), BF16),
        in_specs=[vmem_spec, vmem_spec],
        out_specs=vmem_spec,
    )(position_of.reshape(1, count), items)
    gr, gc = lax.axis_index("gr"), lax.axis_index("gc")
    yh, z = gr // 4, gr % 4
    x, yl, core = gc // 4, (gc // 2) % 2, gc % 2

    def row_at(dx=0, dy=0, dc=0):
        return ((x + dx + 4) % 4) * 4 + ((yl + dy) % 2) * 2 + (core + dc) % 2

    def col_at(dy=0, dz=0):
        return ((yh + dy) % 2) * 4 + (z + dz + 4) % 4

    ring = 1 - 2 * core
    rows_at = [
        [row_at(), row_at(dc=1), row_at(-ring), row_at(ring)],
        [row_at(dy=1), row_at(dy=1, dc=1), row_at(ring, dc=1), row_at(-ring, dc=1)],
        [row_at(2), row_at(-ring, 1, 1), row_at(2, dc=1), row_at(ring, 1)],
        [row_at(-ring, 1), row_at(ring, 1, 1), row_at(2, 1), row_at(2, 1, 1)],
    ]
    cols_at = [
        [col_at(), col_at(dz=-ring)],
        [col_at(dz=ring), col_at(dz=2)],
        [col_at(1), col_at(1, -ring)],
        [col_at(1, ring), col_at(1, 2)],
    ]

    def places(rows, cols):
        flat_list = sum([rows_at[r] for r in rows], []) + sum([cols_at[c] for c in cols], [])
        return flat_list

    lists = [
        places([0], [0]),
        places([1], [0]),
        places([0, 1], [1]),
        places([2], [0, 1]),
        places([0, 1, 2], [2]),
        places([3], [0, 1, 2]),
        places([0, 1, 2, 3], [3]),
    ]
    table = jnp.stack([jnp.stack(p + [p[0]] * (18 - len(p))) for p in lists]).astype(jnp.int32)
    packed, table = fence(packed, table)
    where = [(table, n) for n in range(len(lists))]
    arrived = lax.all_to_all(
        packed, AXES, split_axis=0, concat_axis=0, tiled=True
    )
    own = pl.pallas_call(
        place_kernel,
        out_shape=jax.ShapeDtypeStruct((count, width), BF16),
        in_specs=[vmem_spec],
        out_specs=vmem_spec,
    )(arrived)

    cross, near, over = {"c": 1}, {"yl": 1}, {"yh": 1, "yl": 1}
    up_x, up_z = {"x": "ring"}, {"z": "ring"}
    def swap(value):
        return [send(v, cross) for v in moved([value], [count // 2] * 2)]

    own_c = send(own, cross)
    x_a, z_a, pair = send(own, up_x), send(own, up_z), send(own, near)
    own, own_c = fence(own, own_c)
    x_b, z_b = send(own, {"x": "back"}), send(own, {"z": "back"})
    pair_c = swap(pair)
    own_c, x_a, x_b, z_a, z_b, pair, *pair_c = fence(own_c, x_a, x_b, z_a, z_b, pair, *pair_c)

    (x_ring,) = moved([x_a, *pair_c], [256])
    x_2 = send(x_ring, up_x)
    p_a, far = send(x_a, near), send(pair, over)
    x_a_c, x_b_c = send(x_a, cross), send(x_b, cross)
    out, best_1, rows_1, inv_1, cols_1, col_inv_1 = block_call(
        where[0], [own, own_c, x_a, x_b], [own, z_a], None
    )
    out, best_2, rows_2, inv_2 = block_call(
        where[1], [pair, *pair_c, x_a_c, x_b_c], [cols_1], out, col_inv=[col_inv_1]
    )
    z_a, best_2 = fence(z_a, best_2)
    z_2 = [send(v, up_z) for v in moved([z_a], [count // 2] * 2)]
    x_2, p_a, far, best_2, *z_2 = fence(x_2, p_a, far, best_2, *z_2)

    (z_2,) = moved(z_2, [count])
    f_a, f_2, p_2 = send(far, up_z), send(z_2, {"yh": 1}), send(p_a, up_x)
    x_2_c, p_a_c = fence(send(x_2, cross), send(p_a, cross))
    out, best_1, best_2, cols_2, col_inv_2 = block_call(
        where[2], [rows_1, rows_2], [z_b, z_2], out, row_inv=[inv_1, inv_2], best=[best_1, best_2]
    )
    out, best_3, rows_3, inv_3 = block_call(
        where[3], [x_2, x_2_c], [cols_1, cols_2], out, col_inv=[col_inv_1, col_inv_2]
    )
    far, best_3 = fence(far, best_3)
    f_b = [send(v, {"z": "back"}) for v in moved([far], [3 * count // 4, count // 4])]
    p_2, best_3 = fence(p_2, best_3)
    p_2_c = swap(p_2)
    out, best_1, best_2, best_3, cols_3, col_inv_3 = block_call(
        where[4],
        [rows_1, rows_2, rows_3],
        [far, f_a],
        out,
        row_inv=[inv_1, inv_2, inv_3],
        best=[best_1, best_2, best_3],
    )
    out, best_4, rows_4, inv_4 = block_call(
        where[5],
        [p_a, p_a_c, p_2, *p_2_c],
        [cols_1, cols_2, cols_3],
        out,
        col_inv=[col_inv_1, col_inv_2, col_inv_3],
    )
    out, best, _, _ = block_call(
        where[6],
        [rows_1, rows_2, rows_3, rows_4],
        [*f_b, f_2],
        out,
        row_inv=[inv_1, inv_2, inv_3, inv_4],
        best=[best_1, best_2, best_3, best_4],
        last=True,
    )

    best = jnp.maximum(best, send(best, cross))
    others = [send(best, way) for way in (near, {"x": "even"}, {"yl": 1, "x": "even"})]
    best = jnp.maximum(jnp.maximum(best, others[0]), jnp.maximum(others[1], others[2]))
    best, out = fence(best, store(out))
    best = jnp.maximum(best, send(best, {"x": "odd"}))
    return out, best.reshape(-1)


def solution(mesh):
    return jax.shard_map(
        per_device,
        mesh=mesh,
        in_specs=(P(("gr", "gc"), None), P(("gr", "gc"))),
        out_specs=(P("gr", "gc"), P("gr")),
        check_vma=False,
    )
```

```python
import jax
import jax.numpy as jnp
from jax import lax
from jax.experimental import pallas as pl
from jax.experimental.pallas import tpu as pltpu
from jax.sharding import PartitionSpec as P

AXES = ("gr", "gc")
SIZES = {"yh": 2, "z": 4, "x": 4, "yl": 2, "c": 2}
F32 = jnp.float32
BF16 = jnp.bfloat16
MIB = 1024 * 1024


def coords(d):
    gr, gc = divmod(d, 16)
    return {"yh": gr // 4, "z": gr % 4, "x": gc // 4, "yl": (gc // 2) % 2, "c": gc % 2}


def flat(c):
    return (c["yh"] * 4 + c["z"]) * 16 + c["x"] * 4 + c["yl"] * 2 + c["c"]


def send(value, route):
    pairs = []
    for d in range(128):
        c = coords(d)
        for k, v in route.items():
            if v == "ring":
                v = 1 if c["c"] == 0 else -1
            elif v == "back":
                v = -1 if c["c"] == 0 else 1
            elif v == "even":
                v = 1 if c[k] % 2 == 0 else -1
            elif v == "odd":
                v = 1 if c[k] % 2 == 1 else -1
            c[k] = (c[k] + v) % SIZES[k]
        pairs.append((d, flat(c)))
    return lax.ppermute(value, AXES, pairs)


def pack_kernel(pos_ref, items_ref, out_ref):
    count, width = items_ref.shape
    pos = pos_ref[...]
    dest = lax.broadcasted_iota(jnp.int32, (count, count), 0)
    hit = (pos // count) == dest
    pick = jnp.where(hit, 1.0, 0.0).astype(BF16)
    step = 1024
    for s in range(0, width, step):
        part = jnp.dot(pick, items_ref[:, s : s + step], preferred_element_type=F32)
        out_ref[:, s // 128 : (s + step) // 128, :] = part.reshape(count, 8, 128).astype(BF16)
    slot = jnp.sum(jnp.where(hit, (pos % count).astype(F32), 0.0), axis=1, keepdims=True)
    out_ref[:, width // 128 :, :] = jnp.broadcast_to(slot[:, :, None], (count, 8, 128)).astype(BF16)


def place_kernel(in_ref, out_ref):
    count, width = out_ref.shape
    slot = in_ref[:, width // 128, :].astype(F32)
    lane = lax.broadcasted_iota(jnp.int32, (count, count), 1).astype(F32)
    pick = jnp.where(slot == lane, 1.0, 0.0).astype(BF16)
    step = 1024
    for s in range(0, width, step):
        part = in_ref[:, s // 128 : (s + step) // 128, :].astype(F32).reshape(count, step)
        out_ref[:, s : s + step] = lax.dot_general(
            pick, part.astype(BF16), (((0,), (0,)), ((), ())), preferred_element_type=F32
        ).astype(BF16)


def moved(sources, sizes):
    width = sources[0].shape[1]
    ins, at = [], 0
    for n, s in enumerate(sources):
        ins.append((n, at, at + s.shape[0]))
        at += s.shape[0]
    pieces, at = [], 0
    for m, size in enumerate(sizes):
        for n, lo, hi in ins:
            start, end = max(lo, at), min(hi, at + size)
            if start < end:
                pieces.append((n, start - lo, m, start - at, end - start))
        at += size

    def kernel(*refs):
        src, dst, sems = refs[: len(sources)], refs[len(sources) : -1], refs[-1]
        copies = [
            pltpu.make_async_copy(
                src[n].at[pl.ds(i, rows)], dst[m].at[pl.ds(o, rows)], sems.at[k]
            )
            for k, (n, i, m, o, rows) in enumerate(pieces)
        ]
        for c in copies:
            c.start()
        for c in copies:
            c.wait()

    return pl.pallas_call(
        kernel,
        out_shape=[jax.ShapeDtypeStruct((size, width), BF16) for size in sizes],
        in_specs=[pl.BlockSpec(memory_space=pl.ANY)] * len(sources),
        out_specs=[pl.BlockSpec(memory_space=pltpu.VMEM)] * len(sizes),
        scratch_shapes=[pltpu.SemaphoreType.DMA((len(pieces),))],
        compiler_params=pltpu.CompilerParams(vmem_limit_bytes=2 * MIB),
    )(*sources)


def pick_kernel(core_ref, up_ref, down_ref, out_ref, sem):
    def take(src):
        c = pltpu.make_async_copy(src, out_ref, sem)
        c.start()
        c.wait()

    @pl.when(core_ref[0] == 0)
    def _():
        take(up_ref)

    @pl.when(core_ref[0] != 0)
    def _():
        take(down_ref)


def pick(core, up, down):
    any_spec = pl.BlockSpec(memory_space=pl.ANY)
    return pl.pallas_call(
        pick_kernel,
        out_shape=jax.ShapeDtypeStruct(up.shape, BF16),
        in_specs=[pl.BlockSpec(memory_space=pltpu.SMEM), any_spec, any_spec],
        out_specs=pl.BlockSpec(memory_space=pltpu.VMEM),
        scratch_shapes=[pltpu.SemaphoreType.DMA],
        compiler_params=pltpu.CompilerParams(vmem_limit_bytes=2 * MIB),
    )(core, up, down)


def inverse_norm(ref, start, rows):
    total = jnp.zeros((rows, 128), F32)
    for s in range(0, ref.shape[1], 128):
        part = ref[start : start + rows, s : s + 128].astype(F32)
        total = total + part * part
    return 1.0 / jnp.sqrt(jnp.sum(total, axis=1, keepdims=True) + 1e-06)


def across(column):
    return jnp.transpose(jnp.broadcast_to(column, (128, 128)))[:1, :]


def make_block_kernel(line, row_sizes, col_sizes, fresh_rows, fresh_cols, diagonal, last):
    n_rb, n_cb = sum(row_sizes) // 128, sum(col_sizes) // 128
    tile = 512
    per_tile = tile // 128

    def kernel(*refs):
        refs = list(refs)

        def grab(count):
            return [refs.pop(0) for _ in range(count)]

        (where,) = grab(1)
        row_refs, col_refs = grab(len(row_sizes)), grab(len(col_sizes))
        row_inv = [] if fresh_rows else grab(len(row_sizes))
        col_inv = [] if fresh_cols else grab(len(col_sizes))
        best_in = [] if fresh_rows else grab(len(row_sizes))
        if not diagonal:
            grab(1)
        (out_ref,) = grab(1)
        best_out = grab(1 if fresh_rows or last else len(row_sizes))
        if fresh_rows:
            rows_v, row_inv_out = grab(2)
        if fresh_cols:
            cols_v, col_inv_out = grab(2)
        row_sem, col_sem = refs

        def loads(sources, sizes, target, sems):
            made, at = [], 0
            for n, (ref, size) in enumerate(zip(sources, sizes)):
                c = pltpu.make_async_copy(
                    ref.at[pl.ds(0, size)], target.at[pl.ds(at, size)], sems.at[n]
                )
                c.start()
                made.append((at, c))
                at += size
            return made

        col_loads = loads(col_refs, col_sizes, cols_v, col_sem) if fresh_cols else []
        row_loads = loads(row_refs, row_sizes, rows_v, row_sem) if fresh_rows else []
        for _, c in col_loads:
            c.wait()
        if fresh_cols:
            for lane in range(0, sum(col_sizes), 128):
                col_inv_out[:, lane : lane + 128] = jnp.broadcast_to(
                    across(inverse_norm(cols_v, lane, 128)), (8, 128)
                )
        if fresh_cols:
            groups = [(0, cols_v, col_inv_out)]
        else:
            starts = [sum(col_sizes[:n]) for n in range(len(col_sizes))]
            groups = list(zip(starts, col_refs, col_inv))
        for t in range(n_rb // per_tile):
            if fresh_rows:
                while row_loads and row_loads[0][0] < (t + 1) * tile:
                    row_loads.pop(0)[1].wait()
                source, part, base = rows_v, None, t * tile
            else:
                part, base = t, 0
                source = row_refs[part]
            products = [
                lax.dot_general(
                    source[base : base + tile, :],
                    ref[...],
                    (((1,), (1,)), ((), ())),
                    preferred_element_type=F32,
                )
                for _, ref, _ in groups
            ]
            for k in range(per_tile):
                r = t * per_tile + k
                span = slice(base + 128 * k, base + 128 * k + 128)
                if fresh_rows:
                    inv = jnp.broadcast_to(inverse_norm(rows_v, span.start, 128), (128, 128))
                    row_inv_out[span, :] = inv
                    top = None
                else:
                    inv = row_inv[part][span, :]
                    top = best_in[part][span, :]
                a = where[line, r]
                here = pl.ds(pl.multiple_of(a * 128, 128), 128)
                for (first, ref, inv_ref), product in zip(groups, products):
                    for lane in range(0, ref.shape[0], 128):
                        lanes = slice(lane, lane + 128)
                        scaled = product[128 * k : 128 * k + 128, lanes] * inv * inv_ref[:1, lanes]
                        there = where[line, n_rb + (first + lane) // 128]
                        out_ref[here, pl.ds(pl.multiple_of(there * 128, 128), 128)] = scaled.astype(
                            BF16
                        )
                        if diagonal and r == 0 and first + lane == 0:
                            across_i = lax.broadcasted_iota(jnp.int32, scaled.shape, 1)
                            down_i = lax.broadcasted_iota(jnp.int32, scaled.shape, 0)
                            scaled = jnp.where(across_i == down_i, -2.0, scaled)
                        top = scaled if top is None else jnp.maximum(top, scaled)
                if last:
                    best_out[0][pl.ds(a, 1), :] = across(jnp.max(top, axis=1, keepdims=True))
                elif fresh_rows:
                    best_out[0][span, :] = top
                else:
                    best_out[part][span, :] = top

    return kernel


def block_call(where, rows, cols, out, row_inv=None, col_inv=None, best=None, last=False):
    where, line = where
    fresh_rows, fresh_cols = row_inv is None, col_inv is None
    row_sizes, col_sizes = [r.shape[0] for r in rows], [c.shape[0] for c in cols]
    n_rows, n_cols = sum(row_sizes), sum(col_sizes)
    width = rows[0].shape[1]
    any_spec = pl.BlockSpec(memory_space=pl.ANY)
    vmem_spec = pl.BlockSpec(memory_space=pltpu.VMEM)
    args = [where, *rows, *cols]
    in_specs = [pl.BlockSpec(memory_space=pltpu.SMEM)]
    in_specs += [any_spec if fresh_rows else vmem_spec] * len(rows)
    in_specs += [any_spec if fresh_cols else vmem_spec] * len(cols)
    for extra in (row_inv, col_inv, best):
        if extra is not None:
            args += extra
            in_specs += [vmem_spec] * len(extra)
    aliases = {}
    if out is not None:
        args.append(out)
        in_specs.append(vmem_spec)
        aliases = {len(args) - 1: 0}
    out_shape = [jax.ShapeDtypeStruct((2048, 1024), BF16)]
    if last:
        out_shape.append(jax.ShapeDtypeStruct((16, 128), F32))
    else:
        out_shape += [jax.ShapeDtypeStruct((512, 128), F32)] * (1 if fresh_rows else len(rows))
    if fresh_rows:
        out_shape.append(jax.ShapeDtypeStruct((n_rows, width), BF16))
        out_shape.append(jax.ShapeDtypeStruct((n_rows, 128), F32))
    if fresh_cols:
        out_shape.append(jax.ShapeDtypeStruct((n_cols, width), BF16))
        out_shape.append(jax.ShapeDtypeStruct((8, n_cols), F32))
    return pl.pallas_call(
        make_block_kernel(line, row_sizes, col_sizes, fresh_rows, fresh_cols, out is None, last),
        out_shape=out_shape,
        in_specs=in_specs,
        out_specs=[vmem_spec] * len(out_shape),
        input_output_aliases=aliases,
        scratch_shapes=[
            pltpu.SemaphoreType.DMA((len(rows),)),
            pltpu.SemaphoreType.DMA((len(cols),)),
        ],
        compiler_params=pltpu.CompilerParams(vmem_limit_bytes=VMEM_LIMIT),
        cost_estimate=pl.CostEstimate(
            flops=n_rows * n_cols * width // 4,
            bytes_accessed=2 * n_rows * n_cols,
            transcendentals=0,
        ),
    )(*args)


def store_kernel(held_ref, out_ref, sems):
    rows = held_ref.shape[0] // sems.shape[0]
    copies = [
        pltpu.make_async_copy(
            held_ref.at[pl.ds(rows * n, rows)], out_ref.at[pl.ds(rows * n, rows)], sems.at[n]
        )
        for n in range(sems.shape[0])
    ]
    for c in copies:
        c.start()
    for c in copies:
        c.wait()


def store(held):
    return pl.pallas_call(
        store_kernel,
        out_shape=jax.ShapeDtypeStruct(held.shape, held.dtype),
        in_specs=[pl.BlockSpec(memory_space=pltpu.VMEM)],
        out_specs=pl.BlockSpec(memory_space=pl.ANY),
        scratch_shapes=[pltpu.SemaphoreType.DMA((4,))],
        compiler_params=pltpu.CompilerParams(vmem_limit_bytes=2 * MIB),
        cost_estimate=pl.CostEstimate(
            flops=0, bytes_accessed=2 * held.size * 2, transcendentals=0
        ),
    )(held)


VMEM_LIMIT = 12 * MIB


def fence(*values):
    return lax.optimization_barrier(values)


def per_device(items, position_of):
    count, width = items.shape
    vmem_spec = pl.BlockSpec(memory_space=pltpu.VMEM)
    packed = pl.pallas_call(
        pack_kernel,
        out_shape=jax.ShapeDtypeStruct((count, width // 128 + 8, 128), BF16),
        in_specs=[vmem_spec, vmem_spec],
        out_specs=vmem_spec,
    )(position_of.reshape(1, count), items)
    gr, gc = lax.axis_index("gr"), lax.axis_index("gc")
    yh, z = gr // 4, gr % 4
    x, yl, core = gc // 4, (gc // 2) % 2, gc % 2

    def row_at(dx=0, dy=0, dc=0):
        return ((x + dx + 4) % 4) * 4 + ((yl + dy) % 2) * 2 + (core + dc) % 2

    def col_at(dy=0, dz=0):
        return ((yh + dy) % 2) * 4 + (z + dz + 4) % 4

    ring = 1 - 2 * core
    rows_at = [
        [row_at(), row_at(dc=1), row_at(-ring), row_at(ring)],
        [row_at(dy=1), row_at(dy=1, dc=1), row_at(ring, dc=1), row_at(-ring, dc=1)],
        [row_at(2), row_at(-ring, 1, 1), row_at(2, dc=1), row_at(ring, 1)],
        [row_at(-ring, 1), row_at(ring, 1, 1), row_at(2, 1), row_at(2, 1, 1)],
    ]
    cols_at = [
        [col_at(), col_at(dz=-ring)],
        [col_at(dz=ring), col_at(dz=2)],
        [col_at(1), col_at(1, -ring)],
        [col_at(1, ring), col_at(1, 2)],
    ]

    def places(rows, cols):
        flat_list = sum([rows_at[r] for r in rows], []) + sum([cols_at[c] for c in cols], [])
        return flat_list

    lists = [
        places([0], [0]),
        places([1], [0]),
        places([0, 1], [1]),
        places([2], [0, 1]),
        places([0, 1, 2], [2]),
        places([3], [0, 1, 2]),
        places([0, 1, 2, 3], [3]),
    ]
    table = jnp.stack([jnp.stack(p + [p[0]] * (18 - len(p))) for p in lists]).astype(jnp.int32)
    packed, table = fence(packed, table)
    where = [(table, n) for n in range(len(lists))]
    arrived = lax.all_to_all(
        packed, AXES, split_axis=0, concat_axis=0, tiled=True
    )
    own = pl.pallas_call(
        place_kernel,
        out_shape=jax.ShapeDtypeStruct((count, width), BF16),
        in_specs=[vmem_spec],
        out_specs=vmem_spec,
    )(arrived)

    cross, near, over = {"c": 1}, {"yl": 1}, {"yh": 1, "yl": 1}
    up_x, up_z = {"x": "ring"}, {"z": "ring"}
    def swap(value):
        return [send(v, cross) for v in moved([value], [count // 2] * 2)]

    own_c = send(own, cross)
    x_a, z_a, pair = send(own, up_x), send(own, up_z), send(own, near)
    own, own_c = fence(own, own_c)
    x_b, z_b = send(own, {"x": "back"}), send(own, {"z": "back"})
    pair_c = swap(pair)
    own_c, x_a, x_b, z_a, z_b, pair, *pair_c = fence(own_c, x_a, x_b, z_a, z_b, pair, *pair_c)

    (x_ring,) = moved([x_a, *pair_c], [256])
    x_2 = send(x_ring, up_x)
    p_a, far = send(x_a, near), send(pair, over)
    x_a_c, x_b_c = send(x_a, cross), send(x_b, cross)
    out, best_1, rows_1, inv_1, cols_1, col_inv_1 = block_call(
        where[0], [own, own_c, x_a, x_b], [own, z_a], None
    )
    out, best_2, rows_2, inv_2 = block_call(
        where[1], [pair, *pair_c, x_a_c, x_b_c], [cols_1], out, col_inv=[col_inv_1]
    )
    z_a, best_2 = fence(z_a, best_2)
    z_2 = [send(v, up_z) for v in moved([z_a], [count // 2] * 2)]
    x_2, p_a, far, best_2, *z_2 = fence(x_2, p_a, far, best_2, *z_2)

    (z_2,) = moved(z_2, [count])
    f_a, f_2, p_2 = send(far, up_z), send(z_2, {"yh": 1}), send(p_a, up_x)
    x_2_c, p_a_c = fence(send(x_2, cross), send(p_a, cross))
    out, best_1, best_2, cols_2, col_inv_2 = block_call(
        where[2], [rows_1, rows_2], [z_b, z_2], out, row_inv=[inv_1, inv_2], best=[best_1, best_2]
    )
    out, best_3, rows_3, inv_3 = block_call(
        where[3], [x_2, x_2_c], [cols_1, cols_2], out, col_inv=[col_inv_1, col_inv_2]
    )
    far, best_3 = fence(far, best_3)
    f_b = [send(far, {"z": "back"})]
    p_2, best_3 = fence(p_2, best_3)
    p_2_c = swap(p_2)
    out, best_1, best_2, best_3, cols_3, col_inv_3 = block_call(
        where[4],
        [rows_1, rows_2, rows_3],
        [far, f_a],
        out,
        row_inv=[inv_1, inv_2, inv_3],
        best=[best_1, best_2, best_3],
    )
    out, best_4, rows_4, inv_4 = block_call(
        where[5],
        [p_a, p_a_c, p_2, *p_2_c],
        [cols_1, cols_2, cols_3],
        out,
        col_inv=[col_inv_1, col_inv_2, col_inv_3],
    )
    out, best, _, _ = block_call(
        where[6],
        [rows_1, rows_2, rows_3, rows_4],
        [*f_b, f_2],
        out,
        row_inv=[inv_1, inv_2, inv_3, inv_4],
        best=[best_1, best_2, best_3, best_4],
        last=True,
    )

    best = jnp.maximum(best, send(best, cross))
    others = [send(best, way) for way in (near, {"x": "even"}, {"yl": 1, "x": "even"})]
    best = jnp.maximum(jnp.maximum(best, others[0]), jnp.maximum(others[1], others[2]))
    best, out = fence(best, store(out))
    best = jnp.maximum(best, send(best, {"x": "odd"}))
    return out, best.reshape(-1)


def solution(mesh):
    return jax.shard_map(
        per_device,
        mesh=mesh,
        in_specs=(P(("gr", "gc"), None), P(("gr", "gc"))),
        out_specs=(P("gr", "gc"), P("gr")),
        check_vma=False,
    )
```

```python
import jax
import jax.numpy as jnp
import numpy as np
from jax import lax
from jax.experimental import pallas as pl
from jax.experimental.pallas import tpu as pltpu
from jax.sharding import PartitionSpec as P

AXES = ("gr", "gc")
SIZES = {"yh": 2, "z": 4, "x": 4, "yl": 2, "c": 2}
F32 = jnp.float32
BF16 = jnp.bfloat16
MIB = 1024 * 1024


def coords(d):
    gr, gc = divmod(d, 16)
    return {"yh": gr // 4, "z": gr % 4, "x": gc // 4, "yl": (gc // 2) % 2, "c": gc % 2}


def flat(c):
    return (c["yh"] * 4 + c["z"]) * 16 + c["x"] * 4 + c["yl"] * 2 + c["c"]


def send(value, route):
    pairs = []
    for d in range(128):
        c = coords(d)
        for k, v in route.items():
            if v == "ring":
                v = 1 if c["c"] == 0 else -1
            elif v == "back":
                v = -1 if c["c"] == 0 else 1
            elif v == "even":
                v = 1 if c[k] % 2 == 0 else -1
            elif v == "odd":
                v = 1 if c[k] % 2 == 1 else -1
            c[k] = (c[k] + v) % SIZES[k]
        pairs.append((d, flat(c)))
    return lax.ppermute(value, AXES, pairs)


def pack_kernel(pos_ref, items_ref, out_ref):
    count, width = items_ref.shape
    pos = pos_ref[...]
    dest = lax.broadcasted_iota(jnp.int32, (count, count), 0)
    hit = (pos // count) == dest
    pick = jnp.where(hit, 1.0, 0.0).astype(BF16)
    step = 1024
    for s in range(0, width, step):
        part = jnp.dot(pick, items_ref[:, s : s + step], preferred_element_type=F32)
        out_ref[:, s // 128 : (s + step) // 128, :] = part.reshape(count, 8, 128).astype(BF16)
    slot = jnp.sum(jnp.where(hit, (pos % count).astype(F32), 0.0), axis=1, keepdims=True)
    out_ref[:, width // 128 :, :] = jnp.broadcast_to(slot[:, :, None], (count, 8, 128)).astype(BF16)


def place_kernel(in_ref, out_ref):
    count, width = out_ref.shape
    slot = in_ref[:, width // 128, :].astype(F32)
    lane = lax.broadcasted_iota(jnp.int32, (count, count), 1).astype(F32)
    pick = jnp.where(slot == lane, 1.0, 0.0).astype(BF16)
    step = 1024
    for s in range(0, width, step):
        part = in_ref[:, s // 128 : (s + step) // 128, :].astype(F32).reshape(count, step)
        out_ref[:, s : s + step] = lax.dot_general(
            pick, part.astype(BF16), (((0,), (0,)), ((), ())), preferred_element_type=F32
        ).astype(BF16)


def moved(sources, sizes):
    width = sources[0].shape[1]
    ins, at = [], 0
    for n, s in enumerate(sources):
        ins.append((n, at, at + s.shape[0]))
        at += s.shape[0]
    pieces, at = [], 0
    for m, size in enumerate(sizes):
        for n, lo, hi in ins:
            start, end = max(lo, at), min(hi, at + size)
            if start < end:
                pieces.append((n, start - lo, m, start - at, end - start))
        at += size

    def kernel(*refs):
        src, dst, sems = refs[: len(sources)], refs[len(sources) : -1], refs[-1]
        copies = [
            pltpu.make_async_copy(
                src[n].at[pl.ds(i, rows)], dst[m].at[pl.ds(o, rows)], sems.at[k]
            )
            for k, (n, i, m, o, rows) in enumerate(pieces)
        ]
        for c in copies:
            c.start()
        for c in copies:
            c.wait()

    return pl.pallas_call(
        kernel,
        out_shape=[jax.ShapeDtypeStruct((size, width), BF16) for size in sizes],
        in_specs=[pl.BlockSpec(memory_space=pl.ANY)] * len(sources),
        out_specs=[pl.BlockSpec(memory_space=pltpu.VMEM)] * len(sizes),
        scratch_shapes=[pltpu.SemaphoreType.DMA((len(pieces),))],
        compiler_params=pltpu.CompilerParams(vmem_limit_bytes=2 * MIB),
    )(*sources)


def pick_kernel(core_ref, up_ref, down_ref, out_ref, sem):
    def take(src):
        c = pltpu.make_async_copy(src, out_ref, sem)
        c.start()
        c.wait()

    @pl.when(core_ref[0] == 0)
    def _():
        take(up_ref)

    @pl.when(core_ref[0] != 0)
    def _():
        take(down_ref)


def pick(core, up, down):
    any_spec = pl.BlockSpec(memory_space=pl.ANY)
    return pl.pallas_call(
        pick_kernel,
        out_shape=jax.ShapeDtypeStruct(up.shape, BF16),
        in_specs=[pl.BlockSpec(memory_space=pltpu.SMEM), any_spec, any_spec],
        out_specs=pl.BlockSpec(memory_space=pltpu.VMEM),
        scratch_shapes=[pltpu.SemaphoreType.DMA],
        compiler_params=pltpu.CompilerParams(vmem_limit_bytes=2 * MIB),
    )(core, up, down)


def inverse_norm(ref, start, rows):
    total = jnp.zeros((rows, 128), F32)
    for s in range(0, ref.shape[1], 128):
        part = ref[start : start + rows, s : s + 128].astype(F32)
        total = total + part * part
    return 1.0 / jnp.sqrt(jnp.sum(total, axis=1, keepdims=True) + 1e-06)


def across(column):
    return jnp.transpose(jnp.broadcast_to(column, (128, 128)))[:1, :]


def make_block_kernel(line, row_sizes, col_sizes, fresh_rows, fresh_cols, diagonal, last):
    n_rb, n_cb = sum(row_sizes) // 128, sum(col_sizes) // 128
    tile = 512
    per_tile = tile // 128

    def kernel(*refs):
        refs = list(refs)

        def grab(count):
            return [refs.pop(0) for _ in range(count)]

        (where,) = grab(1)
        row_refs, col_refs = grab(len(row_sizes)), grab(len(col_sizes))
        row_inv = [] if fresh_rows else grab(len(row_sizes))
        col_inv = [] if fresh_cols else grab(len(col_sizes))
        best_in = [] if fresh_rows else grab(len(row_sizes))
        if not diagonal:
            grab(1)
        (out_ref,) = grab(1)
        best_out = grab(1 if fresh_rows or last else len(row_sizes))
        if fresh_rows:
            rows_v, row_inv_out = grab(2)
        if fresh_cols:
            cols_v, col_inv_out = grab(2)
        row_sem, col_sem = refs

        def loads(sources, sizes, target, sems):
            made, at = [], 0
            for n, (ref, size) in enumerate(zip(sources, sizes)):
                c = pltpu.make_async_copy(
                    ref.at[pl.ds(0, size)], target.at[pl.ds(at, size)], sems.at[n]
                )
                c.start()
                made.append((at, c))
                at += size
            return made

        col_loads = loads(col_refs, col_sizes, cols_v, col_sem) if fresh_cols else []
        row_loads = loads(row_refs, row_sizes, rows_v, row_sem) if fresh_rows else []
        for _, c in col_loads:
            c.wait()
        if fresh_cols:
            for lane in range(0, sum(col_sizes), 128):
                col_inv_out[:, lane : lane + 128] = jnp.broadcast_to(
                    across(inverse_norm(cols_v, lane, 128)), (8, 128)
                )
        if fresh_cols:
            groups = [(0, cols_v, col_inv_out)]
        else:
            starts = [sum(col_sizes[:n]) for n in range(len(col_sizes))]
            groups = list(zip(starts, col_refs, col_inv))
        for t in range(n_rb // per_tile):
            if fresh_rows:
                while row_loads and row_loads[0][0] < (t + 1) * tile:
                    row_loads.pop(0)[1].wait()
                source, part, base = rows_v, None, t * tile
            else:
                part, base = t, 0
                source = row_refs[part]
            products = [
                lax.dot_general(
                    source[base : base + tile, :],
                    ref[...],
                    (((1,), (1,)), ((), ())),
                    preferred_element_type=F32,
                )
                for _, ref, _ in groups
            ]
            for k in range(per_tile):
                r = t * per_tile + k
                span = slice(base + 128 * k, base + 128 * k + 128)
                if fresh_rows:
                    inv = jnp.broadcast_to(inverse_norm(rows_v, span.start, 128), (128, 128))
                    row_inv_out[span, :] = inv
                    top = None
                else:
                    inv = row_inv[part][span, :]
                    top = best_in[part][span, :]
                a = where[line, r]
                here = pl.ds(pl.multiple_of(a * 128, 128), 128)
                for (first, ref, inv_ref), product in zip(groups, products):
                    for lane in range(0, ref.shape[0], 128):
                        lanes = slice(lane, lane + 128)
                        scaled = product[128 * k : 128 * k + 128, lanes] * inv * inv_ref[:1, lanes]
                        there = where[line, n_rb + (first + lane) // 128]
                        out_ref[here, pl.ds(pl.multiple_of(there * 128, 128), 128)] = scaled.astype(
                            BF16
                        )
                        if diagonal and r == 0 and first + lane == 0:
                            across_i = lax.broadcasted_iota(jnp.int32, scaled.shape, 1)
                            down_i = lax.broadcasted_iota(jnp.int32, scaled.shape, 0)
                            scaled = jnp.where(across_i == down_i, -2.0, scaled)
                        top = scaled if top is None else jnp.maximum(top, scaled)
                if last:
                    best_out[0][pl.ds(a, 1), :] = across(jnp.max(top, axis=1, keepdims=True))
                elif fresh_rows:
                    best_out[0][span, :] = top
                else:
                    best_out[part][span, :] = top

    return kernel


def block_call(where, rows, cols, out, row_inv=None, col_inv=None, best=None, last=False):
    where, line = where
    fresh_rows, fresh_cols = row_inv is None, col_inv is None
    row_sizes, col_sizes = [r.shape[0] for r in rows], [c.shape[0] for c in cols]
    n_rows, n_cols = sum(row_sizes), sum(col_sizes)
    width = rows[0].shape[1]
    any_spec = pl.BlockSpec(memory_space=pl.ANY)
    vmem_spec = pl.BlockSpec(memory_space=pltpu.VMEM)
    args = [where, *rows, *cols]
    in_specs = [pl.BlockSpec(memory_space=pltpu.SMEM)]
    in_specs += [any_spec if fresh_rows else vmem_spec] * len(rows)
    in_specs += [any_spec if fresh_cols else vmem_spec] * len(cols)
    for extra in (row_inv, col_inv, best):
        if extra is not None:
            args += extra
            in_specs += [vmem_spec] * len(extra)
    aliases = {}
    if out is not None:
        args.append(out)
        in_specs.append(vmem_spec)
        aliases = {len(args) - 1: 0}
    out_shape = [jax.ShapeDtypeStruct((2048, 1024), BF16)]
    if last:
        out_shape.append(jax.ShapeDtypeStruct((16, 128), F32))
    else:
        out_shape += [jax.ShapeDtypeStruct((512, 128), F32)] * (1 if fresh_rows else len(rows))
    if fresh_rows:
        out_shape.append(jax.ShapeDtypeStruct((n_rows, width), BF16))
        out_shape.append(jax.ShapeDtypeStruct((n_rows, 128), F32))
    if fresh_cols:
        out_shape.append(jax.ShapeDtypeStruct((n_cols, width), BF16))
        out_shape.append(jax.ShapeDtypeStruct((8, n_cols), F32))
    return pl.pallas_call(
        make_block_kernel(line, row_sizes, col_sizes, fresh_rows, fresh_cols, out is None, last),
        out_shape=out_shape,
        in_specs=in_specs,
        out_specs=[vmem_spec] * len(out_shape),
        input_output_aliases=aliases,
        scratch_shapes=[
            pltpu.SemaphoreType.DMA((len(rows),)),
            pltpu.SemaphoreType.DMA((len(cols),)),
        ],
        compiler_params=pltpu.CompilerParams(vmem_limit_bytes=VMEM_LIMIT),
        cost_estimate=pl.CostEstimate(
            flops=n_rows * n_cols * width // 4,
            bytes_accessed=2 * n_rows * n_cols,
            transcendentals=0,
        ),
    )(*args)


def store_kernel(held_ref, out_ref, sems):
    rows = held_ref.shape[0] // sems.shape[0]
    copies = [
        pltpu.make_async_copy(
            held_ref.at[pl.ds(rows * n, rows)], out_ref.at[pl.ds(rows * n, rows)], sems.at[n]
        )
        for n in range(sems.shape[0])
    ]
    for c in copies:
        c.start()
    for c in copies:
        c.wait()


def store(held):
    return pl.pallas_call(
        store_kernel,
        out_shape=jax.ShapeDtypeStruct(held.shape, held.dtype),
        in_specs=[pl.BlockSpec(memory_space=pltpu.VMEM)],
        out_specs=pl.BlockSpec(memory_space=pl.ANY),
        scratch_shapes=[pltpu.SemaphoreType.DMA((4,))],
        compiler_params=pltpu.CompilerParams(vmem_limit_bytes=2 * MIB),
        cost_estimate=pl.CostEstimate(
            flops=0, bytes_accessed=2 * held.size * 2, transcendentals=0
        ),
    )(held)


VMEM_LIMIT = 12 * MIB


def fence(*values):
    return lax.optimization_barrier(values)


def per_device(items, position_of):
    count, width = items.shape
    vmem_spec = pl.BlockSpec(memory_space=pltpu.VMEM)
    packed = pl.pallas_call(
        pack_kernel,
        out_shape=jax.ShapeDtypeStruct((count, width // 128 + 8, 128), BF16),
        in_specs=[vmem_spec, vmem_spec],
        out_specs=vmem_spec,
    )(position_of.reshape(1, count), items)
    gr, gc = lax.axis_index("gr"), lax.axis_index("gc")
    yh, z = gr // 4, gr % 4
    x, yl, core = gc // 4, (gc // 2) % 2, gc % 2

    ring = 1 - 2 * core
    rows_at = [
        [(0, 0, 0, 0), (0, 0, 0, 1), (-1, 0, 0, 0), (1, 0, 0, 0)],
        [(0, 0, 1, 0), (0, 0, 1, 1), (1, 0, 0, 1), (-1, 0, 0, 1)],
        [(0, 2, 0, 0), (-1, 0, 1, 1), (0, 2, 0, 1), (1, 0, 1, 0)],
        [(-1, 0, 1, 0), (1, 0, 1, 1), (0, 2, 1, 0), (0, 2, 1, 1)],
    ]
    cols_at = [
        [(0, 0, 0), (-1, 0, 0)],
        [(1, 0, 0), (0, 2, 0)],
        [(0, 0, 1), (-1, 0, 1)],
        [(1, 0, 1), (0, 2, 1)],
    ]
    calls = [
        ([0], [0]),
        ([1], [0]),
        ([0, 1], [1]),
        ([2], [0, 1]),
        ([0, 1, 2], [2]),
        ([3], [0, 1, 2]),
        ([0, 1, 2, 3], [3]),
    ]
    codes = np.zeros((len(calls), 18), np.int32)
    for n, (rows, cols) in enumerate(calls):
        entries = [(0, *w) for r in rows for w in rows_at[r]]
        entries += [(1, *w, 0) for c in cols for w in cols_at[c]]
        for m, (kind, turn, step, over_y, over_c) in enumerate(entries):
            codes[n, m] = kind * 64 + (turn + 1) * 16 + step * 4 + over_y * 2 + over_c
    code = jnp.asarray(codes)
    turn = (code // 16 % 4 - 1) * ring + code // 4 % 4 + 4
    over_y, over_c = code // 2 % 2, code % 2
    table = jnp.where(
        code >= 64,
        ((yh + over_y) % 2) * 4 + (z + turn) % 4,
        ((x + turn) % 4) * 4 + ((yl + over_y) % 2) * 2 + (core + over_c) % 2,
    ).astype(jnp.int32)
    packed, table = fence(packed, table)
    where = [(table, n) for n in range(len(calls))]
    arrived = lax.all_to_all(
        packed, AXES, split_axis=0, concat_axis=0, tiled=True
    )
    own = pl.pallas_call(
        place_kernel,
        out_shape=jax.ShapeDtypeStruct((count, width), BF16),
        in_specs=[vmem_spec],
        out_specs=vmem_spec,
    )(arrived)

    cross, near, over = {"c": 1}, {"yl": 1}, {"yh": 1, "yl": 1}
    up_x, up_z = {"x": "ring"}, {"z": "ring"}
    def swap(value):
        return [send(v, cross) for v in moved([value], [count // 2] * 2)]

    own_c = send(own, cross)
    x_a, z_a, pair = send(own, up_x), send(own, up_z), send(own, near)
    own, own_c = fence(own, own_c)
    x_b, z_b = send(own, {"x": "back"}), send(own, {"z": "back"})
    pair_c = swap(pair)
    own_c, x_a, x_b, z_a, z_b, pair, *pair_c = fence(own_c, x_a, x_b, z_a, z_b, pair, *pair_c)

    (x_ring,) = moved([x_a, *pair_c], [256])
    x_2 = send(x_ring, up_x)
    p_a, far = send(x_a, near), send(pair, over)
    x_a_c, x_b_c = send(x_a, cross), send(x_b, cross)
    out, best_1, rows_1, inv_1, cols_1, col_inv_1 = block_call(
        where[0], [own, own_c, x_a, x_b], [own, z_a], None
    )
    out, best_2, rows_2, inv_2 = block_call(
        where[1], [pair, *pair_c, x_a_c, x_b_c], [cols_1], out, col_inv=[col_inv_1]
    )
    z_a, best_2 = fence(z_a, best_2)
    z_2 = [send(v, up_z) for v in moved([z_a], [count // 2] * 2)]
    x_2, p_a, far, best_2, *z_2 = fence(x_2, p_a, far, best_2, *z_2)

    (z_2,) = moved(z_2, [count])
    f_a, f_2, p_2 = send(far, up_z), send(z_2, {"yh": 1}), send(p_a, up_x)
    x_2_c, p_a_c = fence(send(x_2, cross), send(p_a, cross))
    out, best_1, best_2, cols_2, col_inv_2 = block_call(
        where[2], [rows_1, rows_2], [z_b, z_2], out, row_inv=[inv_1, inv_2], best=[best_1, best_2]
    )
    out, best_3, rows_3, inv_3 = block_call(
        where[3], [x_2, x_2_c], [cols_1, cols_2], out, col_inv=[col_inv_1, col_inv_2]
    )
    far, best_3 = fence(far, best_3)
    f_b = [send(far, {"z": "back"})]
    p_2, best_3 = fence(p_2, best_3)
    p_2_c = swap(p_2)
    out, best_1, best_2, best_3, cols_3, col_inv_3 = block_call(
        where[4],
        [rows_1, rows_2, rows_3],
        [far, f_a],
        out,
        row_inv=[inv_1, inv_2, inv_3],
        best=[best_1, best_2, best_3],
    )
    out, best_4, rows_4, inv_4 = block_call(
        where[5],
        [p_a, p_a_c, p_2, *p_2_c],
        [cols_1, cols_2, cols_3],
        out,
        col_inv=[col_inv_1, col_inv_2, col_inv_3],
    )
    out, best, _, _ = block_call(
        where[6],
        [rows_1, rows_2, rows_3, rows_4],
        [*f_b, f_2],
        out,
        row_inv=[inv_1, inv_2, inv_3, inv_4],
        best=[best_1, best_2, best_3, best_4],
        last=True,
    )

    best = jnp.maximum(best, send(best, cross))
    others = [send(best, way) for way in (near, {"x": "even"}, {"yl": 1, "x": "even"})]
    best = jnp.maximum(jnp.maximum(best, others[0]), jnp.maximum(others[1], others[2]))
    best, out = fence(best, store(out))
    best = jnp.maximum(best, send(best, {"x": "odd"}))
    return out, best.reshape(-1)


def solution(mesh):
    return jax.shard_map(
        per_device,
        mesh=mesh,
        in_specs=(P(("gr", "gc"), None), P(("gr", "gc"))),
        out_specs=(P("gr", "gc"), P("gr")),
        check_vma=False,
    )
```
